32 devices in a mesh: replica: 8 (over z, y), fsdp: 4 (over x, core).
Axes of the slice: x: 2, y: 2, z: 4, core: 2. Of those that a mesh axis runs over, the one named last changes fastest.
Arguments:
- local_weights: float32 [8, 5120, 512], P('replica', 'fsdp')
- outer_base: float32 [5120, 512], P('fsdp')
- outer_momentum: float32 [5120, 512], P(('fsdp', 'replica')), may hold values from -4 to 4
- batch: bfloat16 [8, 2, 1536, 5120], P('replica', None, 'fsdp'), may hold values from -6 to 6
- cotangent: bfloat16 [8, 2, 1536, 512], P('replica', None, 'fsdp'), may hold values from -6 to 6
- step: int32 [1], replicated, may hold values from 0 to 4095
- plan: int32 [8], replicated, may hold values from 0 to 3
Outputs:
- new_weights: float32 [8, 5120, 512], P('replica', 'fsdp')
- new_base: float32 [5120, 512], P('fsdp')
- new_momentum: float32 [5120, 512], P(('fsdp', 'replica'))
The draws below stay inside these ranges and needn't reach their ends.
All inputs are finite; a program needn't handle non-finite values. Where the reference program divides by a largest or mean magnitude, that divisor is 1e-20 or more.
Results may differ from the reference program's by a relative error of at most 0.0055.
Values may be sent and summed in bfloat16 or wider, within the bound.
A program may use at most 128 MiB of HBM per device.

```python
import jax
import jax.numpy as jnp
from jax import lax

D = 5120
VALUE_WIDTH = 512
HEAD_DIM = 128
FRAGMENTS = 4
SCHED_LEN = 8
INNER = 2
TOK_DEV = 384
TOKENS = 1536
N_REPLICA = 8
N_FSDP = 4


def shared_base(key):
    return jax.random.normal(key, (D, VALUE_WIDTH), jnp.float32)


def draw_outer_base(key, part):
    base_values = shared_base(key)
    return base_values


def draw_local_weights(key, part):
    base_values = shared_base(key)
    key = jax.random.fold_in(key, 12)
    drift = jax.random.normal(key, (N_REPLICA, D, VALUE_WIDTH), jnp.float32)
    return base_values[None] + drift


def with_ends(array, rng, least, high):
    extent = array.shape
    place = [jax.random.randint(jax.random.fold_in(rng, axis), (), 0, extent[axis]) for axis in range(len(extent))]
    array = array.at[tuple(place)].set(least)
    longest = extent.index(max(extent))
    place[longest] = (place[longest] + 1) % extent[longest]
    return array.at[tuple(place)].set(high)


def block_levels(rng, extent, split, low, high):
    def one(dim, shards_of):
        draws = jax.random.uniform(jax.random.fold_in(jax.random.fold_in(rng, 6), dim), (shards_of,), jnp.float32, low / len(split), high / len(split))
        return jnp.repeat(jnp.exp(draws), extent[dim] // shards_of).reshape((-1,) + (1,) * (len(extent) - dim - 1))

    factor_of = one(*split[0])
    for cut in split[1:]:
        factor_of = factor_of * one(*cut)
    return factor_of


def noise(rng, dims, deviation, most, cuts=(), kind=jnp.bfloat16):
    values = deviation * jax.random.normal(rng, dims, jnp.float32)
    if cuts:
        values = values * block_levels(rng, dims, cuts, -0.22, 0.18)
    return jnp.clip(values, -most, most).astype(kind)


def setup_inputs(seed: int = 0) -> dict:
    arg_keys = jax.random.split(jax.random.key(seed), 8)
    return {
        "local_weights": draw_local_weights(jax.random.fold_in(arg_keys[7], 71), 0),
        "outer_base": draw_outer_base(jax.random.fold_in(arg_keys[7], 71), 0),
        "outer_momentum": noise(arg_keys[2], (D, VALUE_WIDTH), 0.3, 4.0, ((0, 32),), jnp.float32),
        "batch": noise(arg_keys[3], (N_REPLICA, INNER, TOKENS, D), 1.0, 6.0, ((0, 8), (2, 4))),
        "cotangent": noise(arg_keys[4], (N_REPLICA, INNER, TOKENS, VALUE_WIDTH), 1.0, 6.0, ((0, 8), (2, 4))),
        "step": jax.random.randint(arg_keys[5], (1,), 0, 4096).astype(jnp.int32),
        "plan": with_ends(jax.random.randint(arg_keys[6], (SCHED_LEN,), 0, FRAGMENTS), jax.random.fold_in(arg_keys[6], 1), 0, FRAGMENTS - 1).astype(jnp.int32),
    }


eps_norm = 1e-06
eps_scale = 1e-06
inner_rate = 0.5
outer_rate = 0.7
outer_decay = 0.9
mix_local = 0.5

def pick_fragment(step, plan):
    position = step[0] % SCHED_LEN
    hits = jnp.arange(SCHED_LEN, dtype=jnp.int32) == position
    return jnp.sum(jnp.where(hits, plan, 0)).astype(jnp.int32)

def rate_of(step):
    return outer_rate * 1024.0 / (1024.0 + step[0].astype(jnp.float32))

def normalize(rows):
    values = rows.astype(jnp.float32)
    mean_square = lax.optimization_barrier(jnp.mean(values * values, axis=-1, keepdims=True))
    return (values * lax.rsqrt(mean_square + eps_norm)).astype(jnp.bfloat16)

def silu_slope(values):
    gate_value = jax.nn.sigmoid(values)
    return gate_value * (1.0 + values * (1.0 - gate_value))

def inner_step(weights, batch_rows, cot_rows):
    inv_width = D ** (-0.5)
    normed = normalize(batch_rows)
    values = jnp.dot(normed, weights.astype(jnp.bfloat16), preferred_element_type=jnp.float32) * inv_width
    slopes = (cot_rows.astype(jnp.float32) * silu_slope(values)).astype(jnp.bfloat16)
    normed_groups = normed.reshape(N_FSDP, TOK_DEV, D)
    slope_groups = slopes.reshape(N_FSDP, TOK_DEV, VALUE_WIDTH)

    def add_group(running, pair):
        product = jnp.dot(pair[0].T, pair[1], preferred_element_type=jnp.float32).astype(jnp.bfloat16)
        product = lax.optimization_barrier(product)
        return (running + product.astype(jnp.float32), None)
    gradient, _ = lax.scan(add_group, jnp.zeros((D, VALUE_WIDTH), jnp.float32), (normed_groups, slope_groups))
    return weights - inner_rate * inv_width * gradient

def reference(local_weights, outer_base, outer_momentum, batch, cotangent, step, plan):
    fragment = pick_fragment(step, plan)
    outer_lr = rate_of(step)
    first_col = (fragment * HEAD_DIM).astype(jnp.int32)
    base_cols = lax.dynamic_slice_in_dim(outer_base, first_col, HEAD_DIM, 1)

    def add_replica(running, weights):
        pseudo_grad = base_cols - lax.dynamic_slice_in_dim(weights, first_col, HEAD_DIM, 1)
        block_scale = (lax.optimization_barrier(jnp.max(jnp.abs(pseudo_grad), axis=1, keepdims=True)) + eps_scale).astype(jnp.bfloat16)
        codes = (pseudo_grad / block_scale.astype(jnp.float32)).astype(jnp.bfloat16)
        return (running + codes.astype(jnp.float32) * block_scale.astype(jnp.float32), None)
    running, _ = lax.scan(add_replica, jnp.zeros((D, HEAD_DIM), jnp.float32), local_weights)
    average = running / N_REPLICA
    moment_cols = lax.dynamic_slice_in_dim(outer_momentum, first_col, HEAD_DIM, 1)
    moment_new = outer_decay * moment_cols + average
    base_frag = base_cols - outer_lr * (outer_decay * moment_new + average)
    new_base = lax.dynamic_update_slice_in_dim(outer_base, base_frag, first_col, 1)
    new_momentum = lax.dynamic_update_slice_in_dim(outer_momentum, moment_new, first_col, 1)

    def train(inputs):
        weights, batch_steps, cot_steps = inputs
        for index in range(INNER):
            weights = inner_step(weights, batch_steps[index], cot_steps[index])
        return weights
    trained = lax.map(train, (local_weights, batch, cotangent))
    trained_cols = lax.dynamic_slice_in_dim(trained, first_col, HEAD_DIM, 2)
    blended = mix_local * trained_cols + (1.0 - mix_local) * base_frag[None]
    new_weights = lax.dynamic_update_slice_in_dim(trained, blended, first_col, 2)
    return (new_weights, new_base, new_momentum)
```

```python
import jax
import jax.numpy as jnp
from jax import lax
from jax.experimental import pallas as pl
from jax.experimental.pallas import tpu as pltpu
from jax.sharding import PartitionSpec as P

D = 5120
HEAD_DIM = 128
SCHED_LEN = 8
INNER = 2
MESH = pl.DeviceIdType.MESH


eps_norm = 1e-06
eps_scale = 1e-06
inner_rate = 0.5
outer_rate = 0.7
outer_decay = 0.9
mix_local = 0.5


def pick_fragment(step, plan):
    position = step[0] % SCHED_LEN
    hits = jnp.arange(SCHED_LEN, dtype=jnp.int32) == position
    return jnp.sum(jnp.where(hits, plan, 0))


def rate_of(step):
    return outer_rate * 1024.0 / (1024.0 + step[0].astype(jnp.float32))


def normalize(rows):
    values = rows.astype(jnp.float32)
    mean_square = jnp.mean(values * values, axis=-1, keepdims=True)
    return (values * lax.rsqrt(mean_square + eps_norm)).astype(jnp.bfloat16)


def silu_slope(values):
    gate_value = jax.nn.sigmoid(values)
    return gate_value * (1.0 + values * (1.0 - gate_value))


def on_device(local_weights, outer_base, outer_momentum, batch, cotangent, step, plan):
    inv_width = D ** (-0.5)
    fragment = pick_fragment(step, plan)
    outer_lr = rate_of(step)
    first_col = fragment * HEAD_DIM
    weights = local_weights[0]
    base_cols = lax.dynamic_slice_in_dim(outer_base, first_col, HEAD_DIM, 1)
    pseudo_grad = base_cols - lax.dynamic_slice_in_dim(weights, first_col, HEAD_DIM, 1)
    block_scale = (jnp.max(jnp.abs(pseudo_grad), axis=1) + eps_scale).astype(jnp.bfloat16)
    codes_out = (pseudo_grad / block_scale.astype(jnp.float32)[:, None]).astype(jnp.bfloat16)
    moment_cols = lax.dynamic_slice_in_dim(outer_momentum, first_col, HEAD_DIM, 1)
    share_rows = moment_cols.shape[0]
    share_first = lax.axis_index("replica") * share_rows
    replicas = lax.axis_size("replica")
    dequant = (
        lax.all_gather(codes_out[None], "replica", axis=0, tiled=True).astype(jnp.float32)
        * lax.all_gather(block_scale[None], "replica", axis=0, tiled=True).astype(jnp.float32)[
            :, :, None
        ]
    )
    running = jnp.sum(dequant, axis=0)
    average = running / replicas
    moment_all = lax.all_gather(moment_cols, "replica", axis=0, tiled=True)
    moment_full = outer_decay * moment_all + average
    base_frag = base_cols - outer_lr * (outer_decay * moment_full + average)
    moment_new = lax.dynamic_slice_in_dim(moment_full, share_first, share_rows, 0)
    for index in range(INNER):
        normed = normalize(batch[0, index])
        cot_rows = cotangent[0, index].astype(jnp.float32)
        values = (
            jnp.dot(
                normed,
                lax.all_gather(weights.astype(jnp.bfloat16), "fsdp", axis=0, tiled=True),
                preferred_element_type=jnp.float32,
            )
            * inv_width
        )
        slopes = (cot_rows * silu_slope(values)).astype(jnp.bfloat16)
        gradient = lax.psum_scatter(
            jnp.dot(normed.T, slopes, preferred_element_type=jnp.float32).astype(jnp.bfloat16),
            "fsdp",
            scatter_dimension=0,
            tiled=True,
        ).astype(jnp.float32)
        weights = weights - inner_rate * inv_width * gradient
    trained_cols = lax.dynamic_slice_in_dim(weights, first_col, HEAD_DIM, 1)
    blended = mix_local * trained_cols + (1.0 - mix_local) * base_frag
    new_weights = lax.dynamic_update_slice_in_dim(weights, blended, first_col, 1)[None]
    new_base = lax.dynamic_update_slice_in_dim(outer_base, base_frag, first_col, 1)
    new_momentum = lax.dynamic_update_slice_in_dim(outer_momentum, moment_new, first_col, 1)
    return (new_weights, new_base, new_momentum)


def fused_kernel(
    step_ref, plan_ref, weights_hbm, base_hbm, moment_hbm, batch_hbm, cot_hbm,
    new_weights_hbm, new_base_hbm, new_moment_hbm,
    weights, base, moment, normed, turned, full, cot, slopes,
    part_out, part_in, part_far, part_own, sum_out, sum_in,
    shares, shares_in, frag_rows,
    load_sem, store_sem, gather_send, gather_recv, part_send, part_recv,
    share_send, share_recv, frag_send, frag_recv,
):
    inner, shards, tokens, depth = normed.shape
    halves, width = full.shape[2], full.shape[4]
    replicas, share_rows = shares.shape[0], shares.shape[1]
    inv_width = (shards * depth) ** (-0.5)
    rate = inner_rate * inv_width
    me = lax.axis_index("fsdp")
    my_replica = lax.axis_index("replica")
    chip, core = me // 2, me % 2
    partner = chip * 2 + (1 - core)
    across = (1 - chip) * 2 + core
    diagonal = (1 - chip) * 2 + (1 - core)

    def peer(offset):
        return lax.rem(my_replica + offset, replicas)

    def block_cols(half):
        return pl.ds(half * width, width)

    loads = []

    def load(src, dst):
        copy = pltpu.make_async_copy(src, dst, load_sem.at[len(loads)])
        copy.start()
        loads.append(copy)
        return copy

    load_w = [load(weights_hbm.at[:, block_cols(h)], weights.at[:, block_cols(h)]) for h in range(halves)]
    load_x = [
        [load(batch_hbm.at[k, :, pl.ds(o * depth, depth)], normed.at[k, o]) for o in range(shards)]
        for k in range(inner)
    ]
    load_base = load(base_hbm, base)
    load_moment = load(moment_hbm, moment)
    load_cot = load(cot_hbm, cot)

    barrier = pltpu.get_barrier_semaphore()
    for other in (partner, across):
        pl.semaphore_signal(barrier, inc=1, device_id={"fsdp": other}, device_id_type=MESH)
    for offset in range(1, replicas):
        pl.semaphore_signal(barrier, inc=1, device_id={"replica": peer(offset)}, device_id_type=MESH)
    pl.semaphore_wait(barrier, replicas + 1)

    started = []

    def send(src, dst, send_sem, recv_sem, target):
        copy = pltpu.make_async_remote_copy(
            src_ref=src, dst_ref=dst, send_sem=send_sem, recv_sem=recv_sem,
            device_id=target, device_id_type=MESH,
        )
        copy.start()
        started.append(copy)
        return copy

    def slot(k, h, i):
        return (k * halves + h) * 3 + i

    gathers, partials, sums = {}, {}, {}

    def gather_start(k, h):
        full[k, me, h] = weights[:, h * width : (h + 1) * width].astype(jnp.bfloat16)
        mine = full.at[k, me, h]
        gathers[k, h] = [
            send(mine, mine, gather_send.at[slot(k, h, i)], gather_recv.at[slot(k, h, i)], {"fsdp": target})
            for i, target in enumerate((across, partner))
        ]

    def gather_finish(k, h):
        gathers[k, h][0].wait_recv()
        theirs = full.at[k, across, h]
        forward = send(
            theirs, theirs, gather_send.at[slot(k, h, 2)], gather_recv.at[slot(k, h, 2)], {"fsdp": partner}
        )
        gathers[k, h][1].wait_recv()
        forward.wait_recv()

    def normalize_rows(k):
        rows = 16

        @pl.loop(0, tokens // rows)
        def _(i):
            at = pl.ds(pl.multiple_of(i * rows, rows), rows)
            total = jnp.zeros((rows, 1), jnp.float32)
            for o in range(shards):
                x = normed[k, o, at, :].astype(jnp.float32)
                total = total + jnp.sum(x * x, axis=-1, keepdims=True)
            scale = lax.rsqrt(total * (1.0 / (shards * depth)) + eps_norm)
            for o in range(shards):
                x = normed[k, o, at, :].astype(jnp.float32)
                normed[k, o, at, :] = (x * scale).astype(jnp.bfloat16)

    tile = 256

    def turn(k):
        for o in range(shards):

            @pl.loop(0, depth // tile)
            def _(b):
                at = pl.ds(pl.multiple_of(b * tile, tile), tile)
                turned[o, at, :] = normed[k, o, :, at].T

    def forward(k, h):
        def add(o, total):
            return total + jnp.dot(normed[k, o], full[k, o, h], preferred_element_type=jnp.float32)

        values = lax.fori_loop(0, shards, add, jnp.zeros((tokens, width), jnp.float32)) * inv_width
        cot_rows = cot[k, :, h * width : (h + 1) * width].astype(jnp.float32)
        slopes[...] = (cot_rows * silu_slope(values)).astype(jnp.bfloat16)

    def product(owner, dst):
        @pl.loop(0, depth // tile)
        def _(b):
            at = pl.ds(pl.multiple_of(b * tile, tile), tile)
            dst[at, :] = jnp.dot(
                turned[owner, at, :], slopes[...], preferred_element_type=jnp.float32
            ).astype(jnp.bfloat16)

    def gradient_start(k, h):
        sent = []
        for i, owner in enumerate((diagonal, partner)):
            product(owner, part_out.at[k, h, i])
            sent.append(
                send(
                    part_out.at[k, h, i], part_in.at[k, h, i],
                    part_send.at[slot(k, h, i)], part_recv.at[slot(k, h, i)], {"fsdp": partner},
                )
            )
        partials[k, h] = sent
        product(across, part_far)
        sent[0].wait_recv()
        sum_out[k, h] = (part_far[...].astype(jnp.float32) + part_in[k, h, 0].astype(jnp.float32)).astype(
            jnp.bfloat16
        )
        sums[k, h] = send(
            sum_out.at[k, h], sum_in.at[k, h],
            part_send.at[slot(k, h, 2)], part_recv.at[slot(k, h, 2)], {"fsdp": across},
        )
        product(me, part_own.at[h])

    def gradient_finish(k, h):
        partials[k, h][1].wait_recv()
        sums[k, h].wait_recv()
        gradient = (
            part_own[h].astype(jnp.float32)
            + part_in[k, h, 1].astype(jnp.float32)
            + sum_in[k, h].astype(jnp.float32)
        )
        cols = slice(h * width, (h + 1) * width)
        weights[:, cols] = weights[:, cols] - rate * gradient

    fragment = plan_ref[lax.rem(step_ref[0], SCHED_LEN)]
    fragments = base.shape[1] // HEAD_DIM

    def chosen(rows, index):
        return jnp.full((rows, HEAD_DIM), fragment, jnp.int32) == index

    def pick(ref, at, rows):
        found = ref[at, 0:HEAD_DIM]
        for j in range(1, fragments):
            found = jnp.where(chosen(rows, j), ref[at, j * HEAD_DIM : (j + 1) * HEAD_DIM], found)
        return found

    def share_at(r):
        return pl.ds(pl.multiple_of(r * share_rows, share_rows), share_rows)

    def share_start():
        @pl.loop(0, replicas)
        def _(r):
            at = share_at(r)
            pseudo_grad = pick(base, at, share_rows) - pick(weights, at, share_rows)
            top = jnp.max(jnp.abs(pseudo_grad), axis=1, keepdims=True) + eps_scale
            scale = jnp.broadcast_to(top, pseudo_grad.shape).astype(jnp.bfloat16).astype(jnp.float32)
            codes = (pseudo_grad / scale).astype(jnp.bfloat16).astype(jnp.float32)
            shares[r] = codes * scale

        return [
            send(
                shares.at[peer(t)], shares_in.at[t - 1],
                share_send.at[t - 1], share_recv.at[t - 1], {"replica": peer(t)},
            )
            for t in range(1, replicas)
        ]

    def fragment_start(sent):
        running = shares[my_replica]
        for t in range(1, replicas):
            sent[t - 1].wait_recv()
            running = running + shares_in[t - 1]
        average = running / replicas
        outer_lr = (outer_rate * 1024.0) / (
            1024.0 + jnp.full((share_rows, HEAD_DIM), step_ref[0], jnp.int32).astype(jnp.float32)
        )
        everything = slice(0, share_rows)
        moment_new = outer_decay * pick(moment, everything, share_rows) + average
        frag_rows[my_replica] = pick(base, share_at(my_replica), share_rows) - outer_lr * (
            outer_decay * moment_new + average
        )
        for j in range(fragments):
            cols = slice(j * HEAD_DIM, (j + 1) * HEAD_DIM)
            moment[:, cols] = jnp.where(chosen(share_rows, j), moment_new, moment[:, cols])
        return [
            send(
                frag_rows.at[my_replica], frag_rows.at[my_replica],
                frag_send.at[t - 1], frag_recv.at[t - 1], {"replica": peer(t)},
            )
            for t in range(1, replicas)
        ]

    def fragment_finish(sent):
        for copy in sent:
            copy.wait_recv()

        @pl.loop(0, replicas)
        def _(r):
            at = share_at(r)
            for j in range(fragments):
                cols = slice(j * HEAD_DIM, (j + 1) * HEAD_DIM)
                base[at, cols] = jnp.where(chosen(share_rows, j), frag_rows[r], base[at, cols])

    def blend(h):
        @pl.loop(0, replicas)
        def _(r):
            at = share_at(r)
            for j in range(h * width // HEAD_DIM, (h + 1) * width // HEAD_DIM):
                cols = slice(j * HEAD_DIM, (j + 1) * HEAD_DIM)
                trained = weights[at, cols]
                mixed = mix_local * trained + (1.0 - mix_local) * frag_rows[r]
                weights[at, cols] = jnp.where(chosen(share_rows, j), mixed, trained)

    for h in range(halves):
        load_w[h].wait()
        gather_start(0, h)
    load_base.wait()
    share_sent = share_start()
    frag_sent = None
    stores = []
    for k in range(inner):
        if k == 0:
            for copy in load_x[0]:
                copy.wait()
            normalize_rows(0)
            turn(0)
            load_cot.wait()
        for h in range(halves):
            gather_finish(k, h)
            forward(k, h)
            gradient_start(k, h)
            if k == 0 and h == 0:
                for copy in load_x[1]:
                    copy.wait()
                normalize_rows(1)
        if k + 1 < inner:
            turn(k + 1)
        if k == 0:
            load_moment.wait()
            frag_sent = fragment_start(share_sent)
        for h in range(halves):
            gradient_finish(k, h)
            if k + 1 < inner:
                gather_start(k + 1, h)
            else:
                blend(h)
                copy = pltpu.make_async_copy(
                    weights.at[:, block_cols(h)], new_weights_hbm.at[:, block_cols(h)], store_sem.at[h]
                )
                copy.start()
                stores.append(copy)
        if k == 0:
            fragment_finish(frag_sent)
            for i, (src, dst) in enumerate(((base, new_base_hbm), (moment, new_moment_hbm))):
                copy = pltpu.make_async_copy(src, dst, store_sem.at[halves + i])
                copy.start()
                stores.append(copy)
    for copy in started:
        copy.wait_send()
    for copy in stores:
        copy.wait()


def fused(local_weights, outer_base, outer_momentum, batch, cotangent, step, plan):
    rows, columns = outer_base.shape
    inner, tokens, features = batch.shape[1:]
    shards, replicas = features // rows, rows // outer_momentum.shape[0]
    share_rows = outer_momentum.shape[0]
    halves = 2
    width = columns // halves
    f32, bf16 = jnp.float32, jnp.bfloat16
    hbm = pl.BlockSpec(memory_space=pl.ANY)
    smem = pl.BlockSpec(memory_space=pltpu.SMEM)
    dma = pltpu.SemaphoreType.DMA
    flops = inner * 4 * tokens * features * columns
    return pl.pallas_call(
        fused_kernel,
        out_shape=(
            jax.ShapeDtypeStruct((rows, columns), f32),
            jax.ShapeDtypeStruct((rows, columns), f32),
            jax.ShapeDtypeStruct((share_rows, columns), f32),
        ),
        in_specs=[smem, smem] + [hbm] * 5,
        out_specs=(hbm,) * 3,
        scratch_shapes=[
            pltpu.VMEM((rows, columns), f32),
            pltpu.VMEM((rows, columns), f32),
            pltpu.VMEM((share_rows, columns), f32),
            pltpu.VMEM((inner, shards, tokens, rows), bf16),
            pltpu.VMEM((shards, rows, tokens), bf16),
            pltpu.VMEM((inner, shards, halves, rows, width), bf16),
            pltpu.VMEM((inner, tokens, columns), bf16),
            pltpu.VMEM((tokens, width), bf16),
            pltpu.VMEM((inner, halves, 2, rows, width), bf16),
            pltpu.VMEM((inner, halves, 2, rows, width), bf16),
            pltpu.VMEM((rows, width), bf16),
            pltpu.VMEM((halves, rows, width), bf16),
            pltpu.VMEM((inner, halves, rows, width), bf16),
            pltpu.VMEM((inner, halves, rows, width), bf16),
            pltpu.VMEM((replicas, share_rows, HEAD_DIM), f32),
            pltpu.VMEM((replicas - 1, share_rows, HEAD_DIM), f32),
            pltpu.VMEM((replicas, share_rows, HEAD_DIM), f32),
            dma((halves + inner * shards + 3,)),
            dma((halves + 2,)),
            dma((inner * halves * 3,)),
            dma((inner * halves * 3,)),
            dma((inner * halves * 3,)),
            dma((inner * halves * 3,)),
            dma((replicas - 1,)),
            dma((replicas - 1,)),
            dma((replicas - 1,)),
            dma((replicas - 1,)),
        ],
        compiler_params=pltpu.CompilerParams(
            collective_id=0, has_side_effects=True, vmem_limit_bytes=60 * 2**20
        ),
        cost_estimate=pl.CostEstimate(
            flops=flops, bytes_accessed=20 * 2**20, transcendentals=inner * tokens * columns
        ),
    )(step, plan, local_weights[0], outer_base, outer_momentum, batch[0], cotangent[0])


def on_device_fused(*args):
    new_weights, new_base, new_momentum = fused(*args)
    return (new_weights[None], new_base, new_momentum)


def fits(mesh):
    shards, replicas = mesh.shape["fsdp"], mesh.shape["replica"]
    return shards == 4 and (D // (shards * replicas)) % 8 == 0


def solution(mesh):
    placed = (
        P("replica", "fsdp", None),
        P("fsdp", None),
        P(("fsdp", "replica"), None),
        P("replica", None, "fsdp", None),
        P("replica", None, "fsdp", None),
        P(),
        P(),
    )
    return jax.shard_map(
        on_device_fused if fits(mesh) else on_device,
        mesh=mesh,
        in_specs=placed,
        out_specs=(P("replica", "fsdp", None), P("fsdp", None), P(("fsdp", "replica"), None)),
        check_vma=False,
    )
```

```python
import jax
import jax.numpy as jnp
from jax import lax
from jax.experimental import pallas as pl
from jax.experimental.pallas import tpu as pltpu
from jax.sharding import PartitionSpec as P

D = 5120
HEAD_DIM = 128
SCHED_LEN = 8
INNER = 2
MESH = pl.DeviceIdType.MESH


eps_norm = 1e-06
eps_scale = 1e-06
inner_rate = 0.5
outer_rate = 0.7
outer_decay = 0.9
mix_local = 0.5


def pick_fragment(step, plan):
    position = step[0] % SCHED_LEN
    hits = jnp.arange(SCHED_LEN, dtype=jnp.int32) == position
    return jnp.sum(jnp.where(hits, plan, 0))


def rate_of(step):
    return outer_rate * 1024.0 / (1024.0 + step[0].astype(jnp.float32))


def normalize(rows):
    values = rows.astype(jnp.float32)
    mean_square = jnp.mean(values * values, axis=-1, keepdims=True)
    return (values * lax.rsqrt(mean_square + eps_norm)).astype(jnp.bfloat16)


def silu_slope(values):
    gate_value = jax.nn.sigmoid(values)
    return gate_value * (1.0 + values * (1.0 - gate_value))


def on_device(local_weights, outer_base, outer_momentum, batch, cotangent, step, plan):
    inv_width = D ** (-0.5)
    fragment = pick_fragment(step, plan)
    outer_lr = rate_of(step)
    first_col = fragment * HEAD_DIM
    weights = local_weights[0]
    base_cols = lax.dynamic_slice_in_dim(outer_base, first_col, HEAD_DIM, 1)
    pseudo_grad = base_cols - lax.dynamic_slice_in_dim(weights, first_col, HEAD_DIM, 1)
    block_scale = (jnp.max(jnp.abs(pseudo_grad), axis=1) + eps_scale).astype(jnp.bfloat16)
    codes_out = (pseudo_grad / block_scale.astype(jnp.float32)[:, None]).astype(jnp.bfloat16)
    moment_cols = lax.dynamic_slice_in_dim(outer_momentum, first_col, HEAD_DIM, 1)
    share_rows = moment_cols.shape[0]
    share_first = lax.axis_index("replica") * share_rows
    replicas = lax.axis_size("replica")
    dequant = (
        lax.all_gather(codes_out[None], "replica", axis=0, tiled=True).astype(jnp.float32)
        * lax.all_gather(block_scale[None], "replica", axis=0, tiled=True).astype(jnp.float32)[
            :, :, None
        ]
    )
    running = jnp.sum(dequant, axis=0)
    average = running / replicas
    moment_all = lax.all_gather(moment_cols, "replica", axis=0, tiled=True)
    moment_full = outer_decay * moment_all + average
    base_frag = base_cols - outer_lr * (outer_decay * moment_full + average)
    moment_new = lax.dynamic_slice_in_dim(moment_full, share_first, share_rows, 0)
    for index in range(INNER):
        normed = normalize(batch[0, index])
        cot_rows = cotangent[0, index].astype(jnp.float32)
        values = (
            jnp.dot(
                normed,
                lax.all_gather(weights.astype(jnp.bfloat16), "fsdp", axis=0, tiled=True),
                preferred_element_type=jnp.float32,
            )
            * inv_width
        )
        slopes = (cot_rows * silu_slope(values)).astype(jnp.bfloat16)
        gradient = lax.psum_scatter(
            jnp.dot(normed.T, slopes, preferred_element_type=jnp.float32).astype(jnp.bfloat16),
            "fsdp",
            scatter_dimension=0,
            tiled=True,
        ).astype(jnp.float32)
        weights = weights - inner_rate * inv_width * gradient
    trained_cols = lax.dynamic_slice_in_dim(weights, first_col, HEAD_DIM, 1)
    blended = mix_local * trained_cols + (1.0 - mix_local) * base_frag
    new_weights = lax.dynamic_update_slice_in_dim(weights, blended, first_col, 1)[None]
    new_base = lax.dynamic_update_slice_in_dim(outer_base, base_frag, first_col, 1)
    new_momentum = lax.dynamic_update_slice_in_dim(outer_momentum, moment_new, first_col, 1)
    return (new_weights, new_base, new_momentum)


def fused_kernel(
    step_ref, plan_ref, weights_hbm, base_hbm, moment_hbm, batch_hbm, cot_hbm,
    weights, base, moment,
    normed, turned, full, cot, total, slopes,
    part_out, part_in, part_far, part_own, sum_out, sum_in,
    shares, shares_in, frag_rows,
    load_sem, gather_send, gather_recv, part_send, part_recv,
    share_send, share_recv, frag_send, frag_recv,
):
    inner, shards, tokens, depth = normed.shape
    halves, width = full.shape[2], full.shape[4]
    replicas, share_rows = shares.shape[0], shares.shape[1]
    inv_width = (shards * depth) ** (-0.5)
    rate = inner_rate * inv_width
    me = lax.axis_index("fsdp")
    my_replica = lax.axis_index("replica")
    chip, core = me // 2, me % 2
    partner = chip * 2 + (1 - core)
    across = (1 - chip) * 2 + core
    diagonal = (1 - chip) * 2 + (1 - core)

    def peer(offset):
        return lax.rem(my_replica + offset, replicas)

    def block_cols(half):
        return pl.ds(half * width, width)

    loads = []

    def load(src, dst):
        copy = pltpu.make_async_copy(src, dst, load_sem.at[len(loads)])
        copy.start()
        loads.append(copy)
        return copy

    def load_half(h):
        return load(weights_hbm.at[:, block_cols(h)], weights.at[:, block_cols(h)])

    load_w = [load_half(0)]
    barrier = pltpu.get_barrier_semaphore()
    for other in (partner, across):
        pl.semaphore_signal(barrier, inc=1, device_id={"fsdp": other}, device_id_type=MESH)
    for offset in range(1, replicas):
        pl.semaphore_signal(barrier, inc=1, device_id={"replica": peer(offset)}, device_id_type=MESH)
    load_w += [load_half(h) for h in range(1, halves)]
    load_x = [
        [load(batch_hbm.at[k, :, pl.ds(o * depth, depth)], normed.at[k, o]) for o in range(shards)]
        for k in range(inner)
    ]
    load_base = load(base_hbm, base)
    load_moment = load(moment_hbm, moment)
    load_cot = load(cot_hbm, cot)

    started = []

    def send(src, dst, send_sem, recv_sem, target):
        copy = pltpu.make_async_remote_copy(
            src_ref=src, dst_ref=dst, send_sem=send_sem, recv_sem=recv_sem,
            device_id=target, device_id_type=MESH,
        )
        copy.start()
        started.append(copy)
        return copy

    def slot(k, h, i):
        return (k * halves + h) * 3 + i

    gathers, partials, sums = {}, {}, {}
    first_rows = depth * 3 // 4 // 16 * 16
    pieces = (pl.ds(0, first_rows), pl.ds(first_rows, depth - first_rows))
    last_slot = inner * halves * 3

    def cast_block(k, h):
        full[k, me, h] = weights[:, h * width : (h + 1) * width].astype(jnp.bfloat16)

    def gather_across(k, h, split=False):
        mine = full.at[k, me, h]
        if split:
            parts = [(mine.at[rows, :], at) for rows, at in zip(pieces, (slot(k, h, 0), last_slot))]
        else:
            parts = [(mine, slot(k, h, 0))]
        gathers[k, h, 0] = [
            send(part, part, gather_send.at[at], gather_recv.at[at], {"fsdp": across}) for part, at in parts
        ]

    def gather_beside(k, h):
        mine = full.at[k, me, h]
        at = slot(k, h, 1)
        gathers[k, h, 1] = send(mine, mine, gather_send.at[at], gather_recv.at[at], {"fsdp": partner})

    def normalize_rows(k):
        rows = 16

        @pl.loop(0, tokens // rows)
        def _(i):
            at = pl.ds(pl.multiple_of(i * rows, rows), rows)
            squares = jnp.zeros((rows, 1), jnp.float32)
            for o in range(shards):
                x = normed[k, o, at, :].astype(jnp.float32)
                squares = squares + jnp.sum(x * x, axis=-1, keepdims=True)
            scale = lax.rsqrt(squares * (1.0 / (shards * depth)) + eps_norm)
            for o in range(shards):
                x = normed[k, o, at, :].astype(jnp.float32)
                normed[k, o, at, :] = (x * scale).astype(jnp.bfloat16)

    tile = 256

    def turn(k):
        for o in range(shards):

            @pl.loop(0, depth // tile)
            def _(b):
                at = pl.ds(pl.multiple_of(b * tile, tile), tile)
                turned[o, at, :] = normed[k, o, :, at].T

    def forward(k, h):
        def term(owner):
            return jnp.dot(normed[k, owner], full[k, owner, h], preferred_element_type=jnp.float32)

        for copy in gathers[k, h, 0]:
            copy.wait_recv()
        theirs = full.at[k, across, h]
        at = slot(k, h, 2)
        passed = send(theirs, theirs, gather_send.at[at], gather_recv.at[at], {"fsdp": partner})
        total[...] = term(me)
        gathers[k, h, 1].wait_recv()
        total[...] += term(partner)
        total[...] += term(across)
        passed.wait_recv()
        values = (total[...] + term(diagonal)) * inv_width
        cot_rows = cot[k, :, h * width : (h + 1) * width].astype(jnp.float32)
        slopes[...] = (cot_rows * silu_slope(values)).astype(jnp.bfloat16)

    def product(owner, dst):
        @pl.loop(0, depth // tile)
        def _(b):
            at = pl.ds(pl.multiple_of(b * tile, tile), tile)
            dst[at, :] = jnp.dot(
                turned[owner, at, :], slopes[...], preferred_element_type=jnp.float32
            ).astype(jnp.bfloat16)

    def gradient_start(k, h):
        sent = []
        for i, owner in enumerate((diagonal, partner)):
            product(owner, part_out.at[k, h, i])
            sent.append(
                send(
                    part_out.at[k, h, i], part_in.at[k, h, i],
                    part_send.at[slot(k, h, i)], part_recv.at[slot(k, h, i)], {"fsdp": partner},
                )
            )
        partials[k, h] = sent
        product(across, part_far)
        sent[0].wait_recv()
        sum_out[k, h] = (part_far[...].astype(jnp.float32) + part_in[k, h, 0].astype(jnp.float32)).astype(
            jnp.bfloat16
        )
        sums[k, h] = send(
            sum_out.at[k, h], sum_in.at[k, h],
            part_send.at[slot(k, h, 2)], part_recv.at[slot(k, h, 2)], {"fsdp": across},
        )
        product(me, part_own.at[h])

    def gradient_finish(k, h):
        partials[k, h][1].wait_recv()
        cols = slice(h * width, (h + 1) * width)
        near = part_own[h].astype(jnp.float32) + part_in[k, h, 1].astype(jnp.float32)
        weights[:, cols] = weights[:, cols] - rate * near
        sums[k, h].wait_recv()
        if k + 1 < inner:
            weights[:, cols] = weights[:, cols] - rate * sum_in[k, h].astype(jnp.float32)
        else:
            blend(h)

    fragment = plan_ref[lax.rem(step_ref[0], SCHED_LEN)]
    fragments = base.shape[1] // HEAD_DIM

    def chosen(rows, index):
        return jnp.full((rows, HEAD_DIM), fragment, jnp.int32) == index

    def pick(ref, at, rows):
        found = ref[at, 0:HEAD_DIM]
        for j in range(1, fragments):
            found = jnp.where(chosen(rows, j), ref[at, j * HEAD_DIM : (j + 1) * HEAD_DIM], found)
        return found

    def share_at(r):
        return pl.ds(pl.multiple_of(r * share_rows, share_rows), share_rows)

    def share_start():
        @pl.loop(0, replicas)
        def _(r):
            at = share_at(r)
            pseudo_grad = pick(base, at, share_rows) - pick(weights, at, share_rows)
            top = jnp.max(jnp.abs(pseudo_grad), axis=1, keepdims=True) + eps_scale
            scale = jnp.broadcast_to(top, pseudo_grad.shape).astype(jnp.bfloat16).astype(jnp.float32)
            codes = (pseudo_grad / scale).astype(jnp.bfloat16).astype(jnp.float32)
            shares[r] = codes * scale

        return [
            send(
                shares.at[peer(t)], shares_in.at[t - 1],
                share_send.at[t - 1], share_recv.at[t - 1], {"replica": peer(t)},
            )
            for t in range(1, replicas)
        ]

    def fragment_start(sent):
        running = shares[my_replica]
        for t in range(1, replicas):
            sent[t - 1].wait_recv()
            running = running + shares_in[t - 1]
        average = running / replicas
        outer_lr = (outer_rate * 1024.0) / (
            1024.0 + jnp.full((share_rows, HEAD_DIM), step_ref[0], jnp.int32).astype(jnp.float32)
        )
        everything = slice(0, share_rows)
        moment_new = outer_decay * pick(moment, everything, share_rows) + average
        frag_rows[my_replica] = pick(base, share_at(my_replica), share_rows) - outer_lr * (
            outer_decay * moment_new + average
        )
        for j in range(fragments):
            cols = slice(j * HEAD_DIM, (j + 1) * HEAD_DIM)
            moment[:, cols] = jnp.where(chosen(share_rows, j), moment_new, moment[:, cols])
        return [
            send(
                frag_rows.at[my_replica], frag_rows.at[my_replica],
                frag_send.at[t - 1], frag_recv.at[t - 1], {"replica": peer(t)},
            )
            for t in range(1, replicas)
        ]

    def fragment_finish(sent):
        for copy in sent:
            copy.wait_recv()

        @pl.loop(0, replicas)
        def _(r):
            at = share_at(r)
            for j in range(fragments):
                cols = slice(j * HEAD_DIM, (j + 1) * HEAD_DIM)
                base[at, cols] = jnp.where(chosen(share_rows, j), frag_rows[r], base[at, cols])

    def blend(h):
        @pl.loop(0, replicas)
        def _(r):
            at = share_at(r)
            for j in range(h * width // HEAD_DIM, (h + 1) * width // HEAD_DIM):
                cols = slice(j * HEAD_DIM, (j + 1) * HEAD_DIM)
                far = sum_in[inner - 1, h, at, j * HEAD_DIM - h * width : (j + 1) * HEAD_DIM - h * width]
                trained = weights[at, cols] - rate * far.astype(jnp.float32)
                mixed = mix_local * trained + (1.0 - mix_local) * frag_rows[r]
                weights[at, cols] = jnp.where(chosen(share_rows, j), mixed, trained)

    load_w[0].wait()
    cast_block(0, 0)
    pl.semaphore_wait(barrier, replicas + 1)
    gather_across(0, 0, split=True)
    gather_beside(0, 0)
    for h in range(1, halves):
        load_w[h].wait()
        cast_block(0, h)
        gather_beside(0, h)
    for copy in load_x[0]:
        copy.wait()
    normalize_rows(0)
    ahead = gathers[0, 0, 0][0]
    ahead.wait_send()
    started.remove(ahead)
    for h in range(1, halves):
        gather_across(0, h)
    load_base.wait()
    share_sent = share_start()
    turn(0)
    load_cot.wait()
    for k in range(inner):
        for h in range(halves):
            forward(k, h)
            gradient_start(k, h)
            if k == 0 and h == 0:
                for copy in load_x[1]:
                    copy.wait()
                normalize_rows(1)
        if k == 0:
            turn(k + 1)
            load_moment.wait()
            frag_sent = fragment_start(share_sent)
        for h in range(halves):
            gradient_finish(k, h)
            if k + 1 < inner:
                cast_block(k + 1, h)
                gather_across(k + 1, h)
                gather_beside(k + 1, h)
        if k == 0:
            fragment_finish(frag_sent)
    for copy in started:
        copy.wait_send()


def store_kernel(weights, base, moment, new_weights, new_base, new_moment, store_sem):
    pairs = ((weights, new_weights), (base, new_base), (moment, new_moment))
    copies = [pltpu.make_async_copy(src, dst, store_sem.at[i]) for i, (src, dst) in enumerate(pairs)]
    for copy in copies:
        copy.start()
    for copy in copies:
        copy.wait()


def store(*results):
    hbm = pl.BlockSpec(memory_space=pltpu.HBM)
    return pl.pallas_call(
        store_kernel,
        out_shape=tuple(jax.ShapeDtypeStruct(x.shape, x.dtype) for x in results),
        in_specs=[pl.BlockSpec(memory_space=pl.ANY)] * 3,
        out_specs=(hbm,) * 3,
        scratch_shapes=[pltpu.SemaphoreType.DMA((3,))],
    )(*results)


def fused(local_weights, outer_base, outer_momentum, batch, cotangent, step, plan):
    rows, columns = outer_base.shape
    inner, tokens, features = batch.shape[1:]
    shards, replicas = features // rows, rows // outer_momentum.shape[0]
    share_rows = outer_momentum.shape[0]
    halves = 2
    width = columns // halves
    f32, bf16 = jnp.float32, jnp.bfloat16
    hbm = pl.BlockSpec(memory_space=pltpu.HBM)
    smem = pl.BlockSpec(memory_space=pltpu.SMEM)
    dma = pltpu.SemaphoreType.DMA
    flops = inner * 4 * tokens * features * columns
    return pl.pallas_call(
        fused_kernel,
        out_shape=(
            pltpu.VMEM((rows, columns), f32),
            pltpu.VMEM((rows, columns), f32),
            pltpu.VMEM((share_rows, columns), f32),
        ),
        in_specs=[smem, smem] + [hbm] * 5,
        out_specs=(pl.BlockSpec(memory_space=pltpu.VMEM),) * 3,
        scratch_shapes=[
            pltpu.VMEM((inner, shards, tokens, rows), bf16),
            pltpu.VMEM((shards, rows, tokens), bf16),
            pltpu.VMEM((inner, shards, halves, rows, width), bf16),
            pltpu.VMEM((inner, tokens, columns), bf16),
            pltpu.VMEM((tokens, width), f32),
            pltpu.VMEM((tokens, width), bf16),
            pltpu.VMEM((inner, halves, 2, rows, width), bf16),
            pltpu.VMEM((inner, halves, 2, rows, width), bf16),
            pltpu.VMEM((rows, width), bf16),
            pltpu.VMEM((halves, rows, width), bf16),
            pltpu.VMEM((inner, halves, rows, width), bf16),
            pltpu.VMEM((inner, halves, rows, width), bf16),
            pltpu.VMEM((replicas, share_rows, HEAD_DIM), f32),
            pltpu.VMEM((replicas - 1, share_rows, HEAD_DIM), f32),
            pltpu.VMEM((replicas, share_rows, HEAD_DIM), f32),
            dma((halves + inner * shards + 3,)),
            dma((inner * halves * 3 + 1,)),
            dma((inner * halves * 3 + 1,)),
            dma((inner * halves * 3,)),
            dma((inner * halves * 3,)),
            dma((replicas - 1,)),
            dma((replicas - 1,)),
            dma((replicas - 1,)),
            dma((replicas - 1,)),
        ],
        compiler_params=pltpu.CompilerParams(
            collective_id=0, has_side_effects=True, vmem_limit_bytes=52 * 2**20
        ),
        cost_estimate=pl.CostEstimate(
            flops=flops, bytes_accessed=20 * 2**20, transcendentals=inner * tokens * columns
        ),
    )(step, plan, local_weights[0], outer_base, outer_momentum, batch[0], cotangent[0])


def on_device_fused(*args):
    new_weights, new_base, new_momentum = store(*fused(*args))
    return (new_weights[None], new_base, new_momentum)


def fits(mesh):
    shards, replicas = mesh.shape["fsdp"], mesh.shape["replica"]
    return shards == 4 and (D // (shards * replicas)) % 8 == 0


def solution(mesh):
    placed = (
        P("replica", "fsdp", None),
        P("fsdp", None),
        P(("fsdp", "replica"), None),
        P("replica", None, "fsdp", None),
        P("replica", None, "fsdp", None),
        P(),
        P(),
    )
    return jax.shard_map(
        on_device_fused if fits(mesh) else on_device,
        mesh=mesh,
        in_specs=placed,
        out_specs=(P("replica", "fsdp", None), P("fsdp", None), P(("fsdp", "replica"), None)),
        check_vma=False,
    )
```

```python
import jax
import jax.numpy as jnp
from jax import lax
from jax.experimental import pallas as pl
from jax.experimental.pallas import tpu as pltpu
from jax.sharding import PartitionSpec as P

D = 5120
HEAD_DIM = 128
SCHED_LEN = 8
INNER = 2
MESH = pl.DeviceIdType.MESH
PIECES = 4


eps_norm = 1e-06
eps_scale = 1e-06
inner_rate = 0.5
outer_rate = 0.7
outer_decay = 0.9
mix_local = 0.5


def pick_fragment(step, plan):
    position = step[0] % SCHED_LEN
    hits = jnp.arange(SCHED_LEN, dtype=jnp.int32) == position
    return jnp.sum(jnp.where(hits, plan, 0))


def rate_of(step):
    return outer_rate * 1024.0 / (1024.0 + step[0].astype(jnp.float32))


def normalize(rows):
    values = rows.astype(jnp.float32)
    mean_square = jnp.mean(values * values, axis=-1, keepdims=True)
    return (values * lax.rsqrt(mean_square + eps_norm)).astype(jnp.bfloat16)


def silu_slope(values):
    gate_value = jax.nn.sigmoid(values)
    return gate_value * (1.0 + values * (1.0 - gate_value))


def on_device(local_weights, outer_base, outer_momentum, batch, cotangent, step, plan):
    inv_width = D ** (-0.5)
    fragment = pick_fragment(step, plan)
    outer_lr = rate_of(step)
    first_col = fragment * HEAD_DIM
    weights = local_weights[0]
    base_cols = lax.dynamic_slice_in_dim(outer_base, first_col, HEAD_DIM, 1)
    pseudo_grad = base_cols - lax.dynamic_slice_in_dim(weights, first_col, HEAD_DIM, 1)
    block_scale = (jnp.max(jnp.abs(pseudo_grad), axis=1) + eps_scale).astype(jnp.bfloat16)
    codes_out = (pseudo_grad / block_scale.astype(jnp.float32)[:, None]).astype(jnp.bfloat16)
    moment_cols = lax.dynamic_slice_in_dim(outer_momentum, first_col, HEAD_DIM, 1)
    share_rows = moment_cols.shape[0]
    share_first = lax.axis_index("replica") * share_rows
    replicas = lax.axis_size("replica")
    dequant = (
        lax.all_gather(codes_out[None], "replica", axis=0, tiled=True).astype(jnp.float32)
        * lax.all_gather(block_scale[None], "replica", axis=0, tiled=True).astype(jnp.float32)[
            :, :, None
        ]
    )
    running = jnp.sum(dequant, axis=0)
    average = running / replicas
    moment_all = lax.all_gather(moment_cols, "replica", axis=0, tiled=True)
    moment_full = outer_decay * moment_all + average
    base_frag = base_cols - outer_lr * (outer_decay * moment_full + average)
    moment_new = lax.dynamic_slice_in_dim(moment_full, share_first, share_rows, 0)
    for index in range(INNER):
        normed = normalize(batch[0, index])
        cot_rows = cotangent[0, index].astype(jnp.float32)
        values = (
            jnp.dot(
                normed,
                lax.all_gather(weights.astype(jnp.bfloat16), "fsdp", axis=0, tiled=True),
                preferred_element_type=jnp.float32,
            )
            * inv_width
        )
        slopes = (cot_rows * silu_slope(values)).astype(jnp.bfloat16)
        gradient = lax.psum_scatter(
            jnp.dot(normed.T, slopes, preferred_element_type=jnp.float32).astype(jnp.bfloat16),
            "fsdp",
            scatter_dimension=0,
            tiled=True,
        ).astype(jnp.float32)
        weights = weights - inner_rate * inv_width * gradient
    trained_cols = lax.dynamic_slice_in_dim(weights, first_col, HEAD_DIM, 1)
    blended = mix_local * trained_cols + (1.0 - mix_local) * base_frag
    new_weights = lax.dynamic_update_slice_in_dim(weights, blended, first_col, 1)[None]
    new_base = lax.dynamic_update_slice_in_dim(outer_base, base_frag, first_col, 1)
    new_momentum = lax.dynamic_update_slice_in_dim(outer_momentum, moment_new, first_col, 1)
    return (new_weights, new_base, new_momentum)


def fused_kernel(
    step_ref, plan_ref, weights_hbm, base_hbm, moment_hbm, batch_hbm, cot_hbm,
    weights, base, moment,
    normed, turned, full, cot, total, slopes,
    part_out, part_in, part_far, part_own, sum_out, sum_in,
    shares, shares_in, frag_rows,
    load_sem, gather_send, gather_recv, across_send, across_recv, pass_send, pass_recv,
    part_send, part_recv, sum_send, sum_recv,
    share_send, share_recv, frag_send, frag_recv,
):
    inner, shards, tokens, depth = normed.shape
    halves, width = full.shape[2], full.shape[4]
    replicas, share_rows = shares.shape[0], shares.shape[1]
    inv_width = (shards * depth) ** (-0.5)
    rate = inner_rate * inv_width
    me = lax.axis_index("fsdp")
    my_replica = lax.axis_index("replica")
    chip, core = me // 2, me % 2
    partner = chip * 2 + (1 - core)
    across = (1 - chip) * 2 + core
    diagonal = (1 - chip) * 2 + (1 - core)

    def peer(offset):
        return lax.rem(my_replica + offset, replicas)

    def block_cols(half):
        return pl.ds(half * width, width)

    loads = []

    def load(src, dst):
        copy = pltpu.make_async_copy(src, dst, load_sem.at[len(loads)])
        copy.start()
        loads.append(copy)
        return copy

    def load_half(h):
        return load(weights_hbm.at[:, block_cols(h)], weights.at[:, block_cols(h)])

    load_w = [load_half(0)]
    barrier = pltpu.get_barrier_semaphore()
    for other in (partner, across):
        pl.semaphore_signal(barrier, inc=1, device_id={"fsdp": other}, device_id_type=MESH)
    for offset in range(1, replicas):
        pl.semaphore_signal(barrier, inc=1, device_id={"replica": peer(offset)}, device_id_type=MESH)
    load_w += [load_half(h) for h in range(1, halves)]
    load_x = [
        [load(batch_hbm.at[k, :, pl.ds(o * depth, depth)], normed.at[k, o]) for o in range(shards)]
        for k in range(inner)
    ]
    load_base = load(base_hbm, base)
    load_moment = load(moment_hbm, moment)
    load_cot = load(cot_hbm, cot)

    started = []

    def send(src, dst, send_sem, recv_sem, target):
        copy = pltpu.make_async_remote_copy(
            src_ref=src, dst_ref=dst, send_sem=send_sem, recv_sem=recv_sem,
            device_id=target, device_id_type=MESH,
        )
        copy.start()
        started.append(copy)
        return copy

    def slot(k, h, i):
        return (k * halves + h) * 2 + i

    gathers, partials, sums = {}, {}, {}
    piece_rows = depth // PIECES
    pieces = [slice(i * piece_rows, (i + 1) * piece_rows) for i in range(PIECES)]

    def piece_slot(k, h, i):
        return (k * halves + h) * PIECES + i

    def cast_rows(k, h, rows):
        full[k, me, h, rows, :] = weights[rows, h * width : (h + 1) * width].astype(jnp.bfloat16)

    def gather_across(k, h, i):
        mine = full.at[k, me, h, pl.ds(i * piece_rows, piece_rows), :]
        at = piece_slot(k, h, i)
        gathers[k, h, "across", i] = send(mine, mine, across_send.at[at], across_recv.at[at], {"fsdp": across})

    def gather_beside(k, h):
        mine = full.at[k, me, h]
        at = k * halves + h
        gathers[k, h, "beside"] = send(mine, mine, gather_send.at[at], gather_recv.at[at], {"fsdp": partner})

    def normalize_rows(k):
        rows = 16

        @pl.loop(0, tokens // rows)
        def _(i):
            at = pl.ds(pl.multiple_of(i * rows, rows), rows)
            squares = jnp.zeros((rows, 1), jnp.float32)
            for o in range(shards):
                x = normed[k, o, at, :].astype(jnp.float32)
                squares = squares + jnp.sum(x * x, axis=-1, keepdims=True)
            scale = lax.rsqrt(squares * (1.0 / (shards * depth)) + eps_norm)
            for o in range(shards):
                x = normed[k, o, at, :].astype(jnp.float32)
                normed[k, o, at, :] = (x * scale).astype(jnp.bfloat16)

    tile = 256

    def turn(k):
        for o in range(shards):

            @pl.loop(0, depth // tile)
            def _(b):
                at = pl.ds(pl.multiple_of(b * tile, tile), tile)
                turned[o, at, :] = normed[k, o, :, at].T

    def forward(k, h):
        def term(owner):
            return jnp.dot(normed[k, owner], full[k, owner, h], preferred_element_type=jnp.float32)

        passed = []
        for i in range(PIECES):
            gathers[k, h, "across", i].wait_recv()
            theirs = full.at[k, across, h, pl.ds(i * piece_rows, piece_rows), :]
            at = piece_slot(k, h, i)
            passed.append(send(theirs, theirs, pass_send.at[at], pass_recv.at[at], {"fsdp": partner}))
        total[...] = term(me)
        gathers[k, h, "beside"].wait_recv()
        total[...] += term(partner)
        total[...] += term(across)
        for copy in passed:
            copy.wait_recv()
        values = (total[...] + term(diagonal)) * inv_width
        cot_rows = cot[k, :, h * width : (h + 1) * width].astype(jnp.float32)
        slopes[...] = (cot_rows * silu_slope(values)).astype(jnp.bfloat16)

    def product(owner, dst):
        @pl.loop(0, depth // tile)
        def _(b):
            at = pl.ds(pl.multiple_of(b * tile, tile), tile)
            dst[at, :] = jnp.dot(
                turned[owner, at, :], slopes[...], preferred_element_type=jnp.float32
            ).astype(jnp.bfloat16)

    def gradient_start(k, h):
        sent = []
        for i, owner in enumerate((diagonal, partner)):
            product(owner, part_out.at[k, h, i])
            sent.append(
                send(
                    part_out.at[k, h, i], part_in.at[k, h, i],
                    part_send.at[slot(k, h, i)], part_recv.at[slot(k, h, i)], {"fsdp": partner},
                )
            )
        partials[k, h] = sent
        product(across, part_far)
        sent[0].wait_recv()
        for i, rows in enumerate(pieces):
            sum_out[k, h, rows, :] = (
                part_far[rows, :].astype(jnp.float32) + part_in[k, h, 0, rows, :].astype(jnp.float32)
            ).astype(jnp.bfloat16)
            piece = pl.ds(i * piece_rows, piece_rows)
            at = piece_slot(k, h, i)
            sums[k, h, i] = send(
                sum_out.at[k, h, piece, :], sum_in.at[k, h, piece, :],
                sum_send.at[at], sum_recv.at[at], {"fsdp": across},
            )
        product(me, part_own.at[h])

    def gradient_finish(k, h):
        partials[k, h][1].wait_recv()
        cols = slice(h * width, (h + 1) * width)
        near = part_own[h].astype(jnp.float32) + part_in[k, h, 1].astype(jnp.float32)
        weights[:, cols] = weights[:, cols] - rate * near
        for i, rows in enumerate(pieces):
            sums[k, h, i].wait_recv()
            if k + 1 < inner:
                weights[rows, cols] = weights[rows, cols] - rate * sum_in[k, h, rows, :].astype(jnp.float32)
                cast_rows(k + 1, h, rows)
                gather_across(k + 1, h, i)
            else:
                blend(h, i)

    fragment = plan_ref[lax.rem(step_ref[0], SCHED_LEN)]
    fragments = base.shape[1] // HEAD_DIM

    def chosen(rows, index):
        return jnp.full((rows, HEAD_DIM), fragment, jnp.int32) == index

    def pick(ref, at, rows):
        found = ref[at, 0:HEAD_DIM]
        for j in range(1, fragments):
            found = jnp.where(chosen(rows, j), ref[at, j * HEAD_DIM : (j + 1) * HEAD_DIM], found)
        return found

    def share_at(r):
        return pl.ds(pl.multiple_of(r * share_rows, share_rows), share_rows)

    def share_start():
        @pl.loop(0, replicas)
        def _(r):
            at = share_at(r)
            pseudo_grad = pick(base, at, share_rows) - pick(weights, at, share_rows)
            top = jnp.max(jnp.abs(pseudo_grad), axis=1, keepdims=True) + eps_scale
            scale = jnp.broadcast_to(top, pseudo_grad.shape).astype(jnp.bfloat16).astype(jnp.float32)
            codes = (pseudo_grad / scale).astype(jnp.bfloat16).astype(jnp.float32)
            shares[r] = codes * scale

        return [
            send(
                shares.at[peer(t)], shares_in.at[t - 1],
                share_send.at[t - 1], share_recv.at[t - 1], {"replica": peer(t)},
            )
            for t in range(1, replicas)
        ]

    def fragment_start(sent):
        running = shares[my_replica]
        for t in range(1, replicas):
            sent[t - 1].wait_recv()
            running = running + shares_in[t - 1]
        average = running / replicas
        outer_lr = (outer_rate * 1024.0) / (
            1024.0 + jnp.full((share_rows, HEAD_DIM), step_ref[0], jnp.int32).astype(jnp.float32)
        )
        everything = slice(0, share_rows)
        moment_new = outer_decay * pick(moment, everything, share_rows) + average
        frag_rows[my_replica] = pick(base, share_at(my_replica), share_rows) - outer_lr * (
            outer_decay * moment_new + average
        )
        for j in range(fragments):
            cols = slice(j * HEAD_DIM, (j + 1) * HEAD_DIM)
            moment[:, cols] = jnp.where(chosen(share_rows, j), moment_new, moment[:, cols])
        return [
            send(
                frag_rows.at[my_replica], frag_rows.at[my_replica],
                frag_send.at[t - 1], frag_recv.at[t - 1], {"replica": peer(t)},
            )
            for t in range(1, replicas)
        ]

    def fragment_finish(sent):
        for copy in sent:
            copy.wait_recv()

        @pl.loop(0, replicas)
        def _(r):
            at = share_at(r)
            for j in range(fragments):
                cols = slice(j * HEAD_DIM, (j + 1) * HEAD_DIM)
                base[at, cols] = jnp.where(chosen(share_rows, j), frag_rows[r], base[at, cols])

    def blend(h, i):
        held = piece_rows // share_rows

        @pl.loop(i * held, (i + 1) * held)
        def _(r):
            at = share_at(r)
            for j in range(h * width // HEAD_DIM, (h + 1) * width // HEAD_DIM):
                cols = slice(j * HEAD_DIM, (j + 1) * HEAD_DIM)
                far = sum_in[inner - 1, h, at, j * HEAD_DIM - h * width : (j + 1) * HEAD_DIM - h * width]
                trained = weights[at, cols] - rate * far.astype(jnp.float32)
                mixed = mix_local * trained + (1.0 - mix_local) * frag_rows[r]
                weights[at, cols] = jnp.where(chosen(share_rows, j), mixed, trained)

    load_w[0].wait()
    cast_rows(0, 0, slice(0, depth))
    pl.semaphore_wait(barrier, replicas + 1)
    for i in range(PIECES):
        gather_across(0, 0, i)
    gather_beside(0, 0)
    for h in range(1, halves):
        load_w[h].wait()
        cast_rows(0, h, slice(0, depth))
        gather_beside(0, h)
    for copy in load_x[0]:
        copy.wait()
    normalize_rows(0)
    for i in range(PIECES // 2):
        ahead = gathers[0, 0, "across", i]
        ahead.wait_send()
        started.remove(ahead)
    for h in range(1, halves):
        for i in range(PIECES):
            gather_across(0, h, i)
    load_base.wait()
    share_sent = share_start()
    turn(0)
    load_cot.wait()
    for k in range(inner):
        for h in range(halves):
            forward(k, h)
            gradient_start(k, h)
            if k == 0 and h == 0:
                for copy in load_x[1]:
                    copy.wait()
                normalize_rows(1)
        if k == 0:
            turn(k + 1)
            load_moment.wait()
            frag_sent = fragment_start(share_sent)
        for h in range(halves):
            gradient_finish(k, h)
            if k + 1 < inner:
                gather_beside(k + 1, h)
        if k == 0:
            fragment_finish(frag_sent)
    for copy in started:
        copy.wait_send()


def store_kernel(weights, base, moment, new_weights, new_base, new_moment, store_sem):
    copies = []

    def start(src, dst):
        copy = pltpu.make_async_copy(src, dst, store_sem.at[len(copies)])
        copy.start()
        copies.append(copy)

    rows = weights.shape[0] // PIECES
    for i in range(PIECES):
        at = pl.ds(i * rows, rows)
        start(weights.at[at, :], new_weights.at[at, :])
        start(base.at[at, :], new_base.at[at, :])
    start(moment, new_moment)
    for copy in copies:
        copy.wait()


def store(*results):
    return pl.pallas_call(
        store_kernel,
        out_shape=tuple(jax.ShapeDtypeStruct(x.shape, x.dtype) for x in results),
        in_specs=[pl.BlockSpec(memory_space=pltpu.VMEM)] * 3,
        out_specs=(pl.BlockSpec(memory_space=pltpu.HBM),) * 3,
        scratch_shapes=[pltpu.SemaphoreType.DMA((2 * PIECES + 1,))],
    )(*results)


def fused(local_weights, outer_base, outer_momentum, batch, cotangent, step, plan):
    rows, columns = outer_base.shape
    inner, tokens, features = batch.shape[1:]
    shards, replicas = features // rows, rows // outer_momentum.shape[0]
    share_rows = outer_momentum.shape[0]
    halves = 2
    width = columns // halves
    f32, bf16 = jnp.float32, jnp.bfloat16
    hbm = pl.BlockSpec(memory_space=pltpu.HBM)
    smem = pl.BlockSpec(memory_space=pltpu.SMEM)
    dma = pltpu.SemaphoreType.DMA
    flops = inner * 4 * tokens * features * columns
    return pl.pallas_call(
        fused_kernel,
        out_shape=(
            pltpu.VMEM((rows, columns), f32),
            pltpu.VMEM((rows, columns), f32),
            pltpu.VMEM((share_rows, columns), f32),
        ),
        in_specs=[smem, smem] + [hbm] * 5,
        out_specs=(pl.BlockSpec(memory_space=pltpu.VMEM),) * 3,
        scratch_shapes=[
            pltpu.VMEM((inner, shards, tokens, rows), bf16),
            pltpu.VMEM((shards, rows, tokens), bf16),
            pltpu.VMEM((inner, shards, halves, rows, width), bf16),
            pltpu.VMEM((inner, tokens, columns), bf16),
            pltpu.VMEM((tokens, width), f32),
            pltpu.VMEM((tokens, width), bf16),
            pltpu.VMEM((inner, halves, 2, rows, width), bf16),
            pltpu.VMEM((inner, halves, 2, rows, width), bf16),
            pltpu.VMEM((rows, width), bf16),
            pltpu.VMEM((halves, rows, width), bf16),
            pltpu.VMEM((inner, halves, rows, width), bf16),
            pltpu.VMEM((inner, halves, rows, width), bf16),
            pltpu.VMEM((replicas, share_rows, HEAD_DIM), f32),
            pltpu.VMEM((replicas - 1, share_rows, HEAD_DIM), f32),
            pltpu.VMEM((replicas, share_rows, HEAD_DIM), f32),
            dma((halves + inner * shards + 3,)),
            dma((inner * halves,)),
            dma((inner * halves,)),
            dma((inner * halves * PIECES,)),
            dma((inner * halves * PIECES,)),
            dma((inner * halves * PIECES,)),
            dma((inner * halves * PIECES,)),
            dma((inner * halves * 2,)),
            dma((inner * halves * 2,)),
            dma((inner * halves * PIECES,)),
            dma((inner * halves * PIECES,)),
            dma((replicas - 1,)),
            dma((replicas - 1,)),
            dma((replicas - 1,)),
            dma((replicas - 1,)),
        ],
        compiler_params=pltpu.CompilerParams(
            collective_id=0, has_side_effects=True, vmem_limit_bytes=52 * 2**20
        ),
        cost_estimate=pl.CostEstimate(
            flops=flops, bytes_accessed=20 * 2**20, transcendentals=inner * tokens * columns
        ),
    )(step, plan, local_weights[0], outer_base, outer_momentum, batch[0], cotangent[0])


def on_device_fused(*args):
    new_weights, new_base, new_momentum = store(*fused(*args))
    return (new_weights[None], new_base, new_momentum)


def fits(mesh):
    shards, replicas = mesh.shape["fsdp"], mesh.shape["replica"]
    return shards == 4 and replicas % PIECES == 0 and (D // (shards * replicas)) % 8 == 0


def solution(mesh):
    placed = (
        P("replica", "fsdp", None),
        P("fsdp", None),
        P(("fsdp", "replica"), None),
        P("replica", None, "fsdp", None),
        P("replica", None, "fsdp", None),
        P(),
        P(),
    )
    return jax.shard_map(
        on_device_fused if fits(mesh) else on_device,
        mesh=mesh,
        in_specs=placed,
        out_specs=(P("replica", "fsdp", None), P("fsdp", None), P(("fsdp", "replica"), None)),
        check_vma=False,
    )
```

```python
import jax
import jax.numpy as jnp
from jax import lax
from jax.experimental import pallas as pl
from jax.experimental.pallas import tpu as pltpu
from jax.sharding import PartitionSpec as P

D = 5120
HEAD_DIM = 128
SCHED_LEN = 8
INNER = 2
MESH = pl.DeviceIdType.MESH
PIECES = 4


eps_norm = 1e-06
eps_scale = 1e-06
inner_rate = 0.5
outer_rate = 0.7
outer_decay = 0.9
mix_local = 0.5


def pick_fragment(step, plan):
    position = step[0] % SCHED_LEN
    hits = jnp.arange(SCHED_LEN, dtype=jnp.int32) == position
    return jnp.sum(jnp.where(hits, plan, 0))


def rate_of(step):
    return outer_rate * 1024.0 / (1024.0 + step[0].astype(jnp.float32))


def normalize(rows):
    values = rows.astype(jnp.float32)
    mean_square = jnp.mean(values * values, axis=-1, keepdims=True)
    return (values * lax.rsqrt(mean_square + eps_norm)).astype(jnp.bfloat16)


def silu_slope(values):
    gate_value = jax.nn.sigmoid(values)
    return gate_value * (1.0 + values * (1.0 - gate_value))


def on_device(local_weights, outer_base, outer_momentum, batch, cotangent, step, plan):
    inv_width = D ** (-0.5)
    fragment = pick_fragment(step, plan)
    outer_lr = rate_of(step)
    first_col = fragment * HEAD_DIM
    weights = local_weights[0]
    base_cols = lax.dynamic_slice_in_dim(outer_base, first_col, HEAD_DIM, 1)
    pseudo_grad = base_cols - lax.dynamic_slice_in_dim(weights, first_col, HEAD_DIM, 1)
    block_scale = (jnp.max(jnp.abs(pseudo_grad), axis=1) + eps_scale).astype(jnp.bfloat16)
    codes_out = (pseudo_grad / block_scale.astype(jnp.float32)[:, None]).astype(jnp.bfloat16)
    moment_cols = lax.dynamic_slice_in_dim(outer_momentum, first_col, HEAD_DIM, 1)
    share_rows = moment_cols.shape[0]
    share_first = lax.axis_index("replica") * share_rows
    replicas = lax.axis_size("replica")
    dequant = (
        lax.all_gather(codes_out[None], "replica", axis=0, tiled=True).astype(jnp.float32)
        * lax.all_gather(block_scale[None], "replica", axis=0, tiled=True).astype(jnp.float32)[
            :, :, None
        ]
    )
    running = jnp.sum(dequant, axis=0)
    average = running / replicas
    moment_all = lax.all_gather(moment_cols, "replica", axis=0, tiled=True)
    moment_full = outer_decay * moment_all + average
    base_frag = base_cols - outer_lr * (outer_decay * moment_full + average)
    moment_new = lax.dynamic_slice_in_dim(moment_full, share_first, share_rows, 0)
    for index in range(INNER):
        normed = normalize(batch[0, index])
        cot_rows = cotangent[0, index].astype(jnp.float32)
        values = (
            jnp.dot(
                normed,
                lax.all_gather(weights.astype(jnp.bfloat16), "fsdp", axis=0, tiled=True),
                preferred_element_type=jnp.float32,
            )
            * inv_width
        )
        slopes = (cot_rows * silu_slope(values)).astype(jnp.bfloat16)
        gradient = lax.psum_scatter(
            jnp.dot(normed.T, slopes, preferred_element_type=jnp.float32).astype(jnp.bfloat16),
            "fsdp",
            scatter_dimension=0,
            tiled=True,
        ).astype(jnp.float32)
        weights = weights - inner_rate * inv_width * gradient
    trained_cols = lax.dynamic_slice_in_dim(weights, first_col, HEAD_DIM, 1)
    blended = mix_local * trained_cols + (1.0 - mix_local) * base_frag
    new_weights = lax.dynamic_update_slice_in_dim(weights, blended, first_col, 1)[None]
    new_base = lax.dynamic_update_slice_in_dim(outer_base, base_frag, first_col, 1)
    new_momentum = lax.dynamic_update_slice_in_dim(outer_momentum, moment_new, first_col, 1)
    return (new_weights, new_base, new_momentum)


def fused_kernel(
    step_hbm, plan_hbm, weights_hbm, base_hbm, moment_hbm, batch_hbm, cot_hbm,
    weights, base, moment,
    step_ref, plan_ref, normed, turned, full, cot, total, slopes,
    part_out, part_in, part_far, part_own, sum_out, sum_in,
    shares, shares_in, frag_rows,
    load_sem, gather_send, gather_recv, across_send, across_recv, pass_send, pass_recv,
    part_send, part_recv, sum_send, sum_recv,
    share_send, share_recv, frag_send, frag_recv,
):
    inner, shards, tokens, depth = normed.shape
    halves, width = full.shape[2], full.shape[4]
    replicas, share_rows = shares.shape[0], shares.shape[1]
    inv_width = (shards * depth) ** (-0.5)
    rate = inner_rate * inv_width
    me = lax.axis_index("fsdp")
    my_replica = lax.axis_index("replica")
    chip, core = me // 2, me % 2
    partner = chip * 2 + (1 - core)
    across = (1 - chip) * 2 + core
    diagonal = (1 - chip) * 2 + (1 - core)

    def peer(offset):
        return lax.rem(my_replica + offset, replicas)

    def block_cols(half):
        return pl.ds(half * width, width)

    loads = []

    def load(src, dst):
        copy = pltpu.make_async_copy(src, dst, load_sem.at[len(loads)])
        copy.start()
        loads.append(copy)
        return copy

    piece_rows = depth // PIECES
    load_first = [
        load(
            weights_hbm.at[pl.ds(i * piece_rows, piece_rows), block_cols(0)],
            weights.at[pl.ds(i * piece_rows, piece_rows), block_cols(0)],
        )
        for i in range(PIECES)
    ]
    barrier = pltpu.get_barrier_semaphore()
    for other in (partner, across):
        pl.semaphore_signal(barrier, inc=1, device_id={"fsdp": other}, device_id_type=MESH)
    for offset in range(1, replicas):
        pl.semaphore_signal(barrier, inc=1, device_id={"replica": peer(offset)}, device_id_type=MESH)
    load_rest = [
        load(weights_hbm.at[:, block_cols(h)], weights.at[:, block_cols(h)]) for h in range(1, halves)
    ]
    load_x = [
        [load(batch_hbm.at[k, :, pl.ds(o * depth, depth)], normed.at[k, o]) for o in range(shards)]
        for k in range(inner)
    ]
    load_base = load(base_hbm, base)
    load_moment = load(moment_hbm, moment)
    load_cot = load(cot_hbm, cot)
    load_small = [load(step_hbm, step_ref), load(plan_hbm, plan_ref)]

    started = []

    def send(src, dst, send_sem, recv_sem, target):
        copy = pltpu.make_async_remote_copy(
            src_ref=src, dst_ref=dst, send_sem=send_sem, recv_sem=recv_sem,
            device_id=target, device_id_type=MESH,
        )
        copy.start()
        started.append(copy)
        return copy

    def slot(k, h, i):
        return (k * halves + h) * 2 + i

    gathers, partials, sums = {}, {}, {}
    pieces = [slice(i * piece_rows, (i + 1) * piece_rows) for i in range(PIECES)]

    def piece_slot(k, h, i):
        return (k * halves + h) * PIECES + i

    def cast_rows(k, h, rows):
        full[k, me, h, rows, :] = weights[rows, h * width : (h + 1) * width].astype(jnp.bfloat16)

    def gather_across(k, h, i):
        mine = full.at[k, me, h, pl.ds(i * piece_rows, piece_rows), :]
        at = piece_slot(k, h, i)
        gathers[k, h, "across", i] = send(mine, mine, across_send.at[at], across_recv.at[at], {"fsdp": across})

    def gather_beside(k, h):
        mine = full.at[k, me, h]
        at = k * halves + h
        gathers[k, h, "beside"] = send(mine, mine, gather_send.at[at], gather_recv.at[at], {"fsdp": partner})

    def normalize_rows(k):
        rows = 16

        @pl.loop(0, tokens // rows)
        def _(i):
            at = pl.ds(pl.multiple_of(i * rows, rows), rows)
            squares = jnp.zeros((rows, 1), jnp.float32)
            for o in range(shards):
                x = normed[k, o, at, :].astype(jnp.float32)
                squares = squares + jnp.sum(x * x, axis=-1, keepdims=True)
            scale = lax.rsqrt(squares * (1.0 / (shards * depth)) + eps_norm)
            for o in range(shards):
                x = normed[k, o, at, :].astype(jnp.float32)
                normed[k, o, at, :] = (x * scale).astype(jnp.bfloat16)

    tile = 256

    def turn(k):
        for o in range(shards):

            @pl.loop(0, depth // tile)
            def _(b):
                at = pl.ds(pl.multiple_of(b * tile, tile), tile)
                turned[o, at, :] = normed[k, o, :, at].T

    def forward(k, h):
        def term(owner):
            return jnp.dot(normed[k, owner], full[k, owner, h], preferred_element_type=jnp.float32)

        passed = []
        for i in range(PIECES):
            gathers[k, h, "across", i].wait_recv()
            theirs = full.at[k, across, h, pl.ds(i * piece_rows, piece_rows), :]
            at = piece_slot(k, h, i)
            passed.append(send(theirs, theirs, pass_send.at[at], pass_recv.at[at], {"fsdp": partner}))
        total[...] = term(me)
        gathers[k, h, "beside"].wait_recv()
        total[...] += term(partner)
        total[...] += term(across)
        for copy in passed:
            copy.wait_recv()
        values = (total[...] + term(diagonal)) * inv_width
        cot_rows = cot[k, :, h * width : (h + 1) * width].astype(jnp.float32)
        slopes[...] = (cot_rows * silu_slope(values)).astype(jnp.bfloat16)

    def product(owner, dst):
        @pl.loop(0, depth // tile)
        def _(b):
            at = pl.ds(pl.multiple_of(b * tile, tile), tile)
            dst[at, :] = jnp.dot(
                turned[owner, at, :], slopes[...], preferred_element_type=jnp.float32
            ).astype(jnp.bfloat16)

    def gradient_start(k, h):
        sent = []
        for i, owner in enumerate((diagonal, partner)):
            product(owner, part_out.at[k, h, i])
            sent.append(
                send(
                    part_out.at[k, h, i], part_in.at[k, h, i],
                    part_send.at[slot(k, h, i)], part_recv.at[slot(k, h, i)], {"fsdp": partner},
                )
            )
        partials[k, h] = sent
        product(across, part_far)
        sent[0].wait_recv()
        for i, rows in enumerate(pieces):
            sum_out[k, h, rows, :] = (
                part_far[rows, :].astype(jnp.float32) + part_in[k, h, 0, rows, :].astype(jnp.float32)
            ).astype(jnp.bfloat16)
            piece = pl.ds(i * piece_rows, piece_rows)
            at = piece_slot(k, h, i)
            sums[k, h, i] = send(
                sum_out.at[k, h, piece, :], sum_in.at[k, h, piece, :],
                sum_send.at[at], sum_recv.at[at], {"fsdp": across},
            )
        product(me, part_own.at[h])

    def gradient_finish(k, h):
        partials[k, h][1].wait_recv()
        cols = slice(h * width, (h + 1) * width)
        near = part_own[h].astype(jnp.float32) + part_in[k, h, 1].astype(jnp.float32)
        weights[:, cols] = weights[:, cols] - rate * near
        for i, rows in enumerate(pieces):
            sums[k, h, i].wait_recv()
            if k + 1 < inner:
                weights[rows, cols] = weights[rows, cols] - rate * sum_in[k, h, rows, :].astype(jnp.float32)
                cast_rows(k + 1, h, rows)
                gather_across(k + 1, h, i)
            else:
                blend(h, i)

    fragments = base.shape[1] // HEAD_DIM

    def chosen(rows, index):
        fragment = plan_ref[lax.rem(step_ref[0], SCHED_LEN)]
        return jnp.full((rows, HEAD_DIM), fragment, jnp.int32) == index

    def pick(ref, at, rows):
        found = ref[at, 0:HEAD_DIM]
        for j in range(1, fragments):
            found = jnp.where(chosen(rows, j), ref[at, j * HEAD_DIM : (j + 1) * HEAD_DIM], found)
        return found

    def share_at(r):
        return pl.ds(pl.multiple_of(r * share_rows, share_rows), share_rows)

    def share_start():
        @pl.loop(0, replicas)
        def _(r):
            at = share_at(r)
            pseudo_grad = pick(base, at, share_rows) - pick(weights, at, share_rows)
            top = jnp.max(jnp.abs(pseudo_grad), axis=1, keepdims=True) + eps_scale
            scale = jnp.broadcast_to(top, pseudo_grad.shape).astype(jnp.bfloat16).astype(jnp.float32)
            codes = (pseudo_grad / scale).astype(jnp.bfloat16).astype(jnp.float32)
            shares[r] = codes * scale

        return [
            send(
                shares.at[peer(t)], shares_in.at[t - 1],
                share_send.at[t - 1], share_recv.at[t - 1], {"replica": peer(t)},
            )
            for t in range(1, replicas)
        ]

    def fragment_start(sent):
        running = shares[my_replica]
        for t in range(1, replicas):
            sent[t - 1].wait_recv()
            running = running + shares_in[t - 1]
        average = running / replicas
        outer_lr = (outer_rate * 1024.0) / (
            1024.0 + jnp.full((share_rows, HEAD_DIM), step_ref[0], jnp.int32).astype(jnp.float32)
        )
        everything = slice(0, share_rows)
        moment_new = outer_decay * pick(moment, everything, share_rows) + average
        frag_rows[my_replica] = pick(base, share_at(my_replica), share_rows) - outer_lr * (
            outer_decay * moment_new + average
        )
        for j in range(fragments):
            cols = slice(j * HEAD_DIM, (j + 1) * HEAD_DIM)
            moment[:, cols] = jnp.where(chosen(share_rows, j), moment_new, moment[:, cols])
        return [
            send(
                frag_rows.at[my_replica], frag_rows.at[my_replica],
                frag_send.at[t - 1], frag_recv.at[t - 1], {"replica": peer(t)},
            )
            for t in range(1, replicas)
        ]

    def fragment_finish(sent):
        for copy in sent:
            copy.wait_recv()

        @pl.loop(0, replicas)
        def _(r):
            at = share_at(r)
            for j in range(fragments):
                cols = slice(j * HEAD_DIM, (j + 1) * HEAD_DIM)
                base[at, cols] = jnp.where(chosen(share_rows, j), frag_rows[r], base[at, cols])

    def blend(h, i):
        held = piece_rows // share_rows

        @pl.loop(i * held, (i + 1) * held)
        def _(r):
            at = share_at(r)
            for j in range(h * width // HEAD_DIM, (h + 1) * width // HEAD_DIM):
                cols = slice(j * HEAD_DIM, (j + 1) * HEAD_DIM)
                far = sum_in[inner - 1, h, at, j * HEAD_DIM - h * width : (j + 1) * HEAD_DIM - h * width]
                trained = weights[at, cols] - rate * far.astype(jnp.float32)
                mixed = mix_local * trained + (1.0 - mix_local) * frag_rows[r]
                weights[at, cols] = jnp.where(chosen(share_rows, j), mixed, trained)

    pl.semaphore_wait(barrier, replicas + 1)
    for i, rows in enumerate(pieces):
        load_first[i].wait()
        cast_rows(0, 0, rows)
        gather_across(0, 0, i)
    gather_beside(0, 0)
    for h in range(1, halves):
        load_rest[h - 1].wait()
        cast_rows(0, h, slice(0, depth))
        gather_beside(0, h)
    for copy in load_x[0]:
        copy.wait()
    normalize_rows(0)
    for i in range(PIECES // 2):
        ahead = gathers[0, 0, "across", i]
        ahead.wait_send()
        started.remove(ahead)
    for h in range(1, halves):
        for i in range(PIECES):
            gather_across(0, h, i)
    turn(0)
    load_cot.wait()
    for k in range(inner):
        for h in range(halves):
            forward(k, h)
            gradient_start(k, h)
            if h > 0:
                continue
            if k == 0:
                for copy in load_x[1]:
                    copy.wait()
                normalize_rows(1)
            else:
                fragment_finish(frag_sent)
        if k == 0:
            for copy in load_small:
                copy.wait()
            load_base.wait()
            share_sent = share_start()
        for h in range(halves):
            gradient_finish(k, h)
            if k + 1 < inner:
                gather_beside(k + 1, h)
            if k == 0 and h == 0:
                turn(1)
        if k == 0:
            load_moment.wait()
            frag_sent = fragment_start(share_sent)
    for copy in started:
        copy.wait_send()


def fused(local_weights, outer_base, outer_momentum, batch, cotangent, step, plan):
    rows, columns = outer_base.shape
    inner, tokens, features = batch.shape[1:]
    shards, replicas = features // rows, rows // outer_momentum.shape[0]
    share_rows = outer_momentum.shape[0]
    halves = 2
    width = columns // halves
    f32, bf16 = jnp.float32, jnp.bfloat16
    hbm = pl.BlockSpec(memory_space=pltpu.HBM)
    dma = pltpu.SemaphoreType.DMA
    flops = inner * 4 * tokens * features * columns
    return pl.pallas_call(
        fused_kernel,
        out_shape=(
            pltpu.VMEM((rows, columns), f32),
            pltpu.VMEM((rows, columns), f32),
            pltpu.VMEM((share_rows, columns), f32),
        ),
        in_specs=[hbm] * 7,
        out_specs=(pl.BlockSpec(memory_space=pltpu.VMEM),) * 3,
        scratch_shapes=[
            pltpu.SMEM(step.shape, jnp.int32),
            pltpu.SMEM(plan.shape, jnp.int32),
            pltpu.VMEM((inner, shards, tokens, rows), bf16),
            pltpu.VMEM((shards, rows, tokens), bf16),
            pltpu.VMEM((inner, shards, halves, rows, width), bf16),
            pltpu.VMEM((inner, tokens, columns), bf16),
            pltpu.VMEM((tokens, width), f32),
            pltpu.VMEM((tokens, width), bf16),
            pltpu.VMEM((inner, halves, 2, rows, width), bf16),
            pltpu.VMEM((inner, halves, 2, rows, width), bf16),
            pltpu.VMEM((rows, width), bf16),
            pltpu.VMEM((halves, rows, width), bf16),
            pltpu.VMEM((inner, halves, rows, width), bf16),
            pltpu.VMEM((inner, halves, rows, width), bf16),
            pltpu.VMEM((replicas, share_rows, HEAD_DIM), f32),
            pltpu.VMEM((replicas - 1, share_rows, HEAD_DIM), f32),
            pltpu.VMEM((replicas, share_rows, HEAD_DIM), f32),
            dma((PIECES + halves - 1 + inner * shards + 5,)),
            dma((inner * halves,)),
            dma((inner * halves,)),
            dma((inner * halves * PIECES,)),
            dma((inner * halves * PIECES,)),
            dma((inner * halves * PIECES,)),
            dma((inner * halves * PIECES,)),
            dma((inner * halves * 2,)),
            dma((inner * halves * 2,)),
            dma((inner * halves * PIECES,)),
            dma((inner * halves * PIECES,)),
            dma((replicas - 1,)),
            dma((replicas - 1,)),
            dma((replicas - 1,)),
            dma((replicas - 1,)),
        ],
        compiler_params=pltpu.CompilerParams(
            collective_id=0, has_side_effects=True, vmem_limit_bytes=52 * 2**20
        ),
        cost_estimate=pl.CostEstimate(
            flops=flops, bytes_accessed=20 * 2**20, transcendentals=inner * tokens * columns
        ),
    )(step, plan, local_weights[0], outer_base, outer_momentum, batch[0], cotangent[0])


def on_device_fused(*args):
    new_weights, new_base, new_momentum = fused(*args)
    return (new_weights[None], new_base, new_momentum)


def fits(mesh):
    shards, replicas = mesh.shape["fsdp"], mesh.shape["replica"]
    return shards == 4 and replicas % PIECES == 0 and (D // (shards * replicas)) % 8 == 0


def solution(mesh):
    placed = (
        P("replica", "fsdp", None),
        P("fsdp", None),
        P(("fsdp", "replica"), None),
        P("replica", None, "fsdp", None),
        P("replica", None, "fsdp", None),
        P(),
        P(),
    )
    return jax.shard_map(
        on_device_fused if fits(mesh) else on_device,
        mesh=mesh,
        in_specs=placed,
        out_specs=(P("replica", "fsdp", None), P("fsdp", None), P(("fsdp", "replica"), None)),
        check_vma=False,
    )
```

```python
import jax
import jax.numpy as jnp
from jax import lax
from jax.experimental import pallas as pl
from jax.experimental.pallas import tpu as pltpu
from jax.sharding import PartitionSpec as P

D = 5120
HEAD_DIM = 128
SCHED_LEN = 8
INNER = 2
MESH = pl.DeviceIdType.MESH
PIECES = 4


eps_norm = 1e-06
eps_scale = 1e-06
inner_rate = 0.5
outer_rate = 0.7
outer_decay = 0.9
mix_local = 0.5


def pick_fragment(step, plan):
    position = step[0] % SCHED_LEN
    hits = jnp.arange(SCHED_LEN, dtype=jnp.int32) == position
    return jnp.sum(jnp.where(hits, plan, 0))


def rate_of(step):
    return outer_rate * 1024.0 / (1024.0 + step[0].astype(jnp.float32))


def normalize(rows):
    values = rows.astype(jnp.float32)
    mean_square = jnp.mean(values * values, axis=-1, keepdims=True)
    return (values * lax.rsqrt(mean_square + eps_norm)).astype(jnp.bfloat16)


def silu_slope(values):
    gate_value = jax.nn.sigmoid(values)
    return gate_value * (1.0 + values * (1.0 - gate_value))


def on_device(local_weights, outer_base, outer_momentum, batch, cotangent, step, plan):
    inv_width = D ** (-0.5)
    fragment = pick_fragment(step, plan)
    outer_lr = rate_of(step)
    first_col = fragment * HEAD_DIM
    weights = local_weights[0]
    base_cols = lax.dynamic_slice_in_dim(outer_base, first_col, HEAD_DIM, 1)
    pseudo_grad = base_cols - lax.dynamic_slice_in_dim(weights, first_col, HEAD_DIM, 1)
    block_scale = (jnp.max(jnp.abs(pseudo_grad), axis=1) + eps_scale).astype(jnp.bfloat16)
    codes_out = (pseudo_grad / block_scale.astype(jnp.float32)[:, None]).astype(jnp.bfloat16)
    moment_cols = lax.dynamic_slice_in_dim(outer_momentum, first_col, HEAD_DIM, 1)
    share_rows = moment_cols.shape[0]
    share_first = lax.axis_index("replica") * share_rows
    replicas = lax.axis_size("replica")
    dequant = (
        lax.all_gather(codes_out[None], "replica", axis=0, tiled=True).astype(jnp.float32)
        * lax.all_gather(block_scale[None], "replica", axis=0, tiled=True).astype(jnp.float32)[
            :, :, None
        ]
    )
    running = jnp.sum(dequant, axis=0)
    average = running / replicas
    moment_all = lax.all_gather(moment_cols, "replica", axis=0, tiled=True)
    moment_full = outer_decay * moment_all + average
    base_frag = base_cols - outer_lr * (outer_decay * moment_full + average)
    moment_new = lax.dynamic_slice_in_dim(moment_full, share_first, share_rows, 0)
    for index in range(INNER):
        normed = normalize(batch[0, index])
        cot_rows = cotangent[0, index].astype(jnp.float32)
        values = (
            jnp.dot(
                normed,
                lax.all_gather(weights.astype(jnp.bfloat16), "fsdp", axis=0, tiled=True),
                preferred_element_type=jnp.float32,
            )
            * inv_width
        )
        slopes = (cot_rows * silu_slope(values)).astype(jnp.bfloat16)
        gradient = lax.psum_scatter(
            jnp.dot(normed.T, slopes, preferred_element_type=jnp.float32).astype(jnp.bfloat16),
            "fsdp",
            scatter_dimension=0,
            tiled=True,
        ).astype(jnp.float32)
        weights = weights - inner_rate * inv_width * gradient
    trained_cols = lax.dynamic_slice_in_dim(weights, first_col, HEAD_DIM, 1)
    blended = mix_local * trained_cols + (1.0 - mix_local) * base_frag
    new_weights = lax.dynamic_update_slice_in_dim(weights, blended, first_col, 1)[None]
    new_base = lax.dynamic_update_slice_in_dim(outer_base, base_frag, first_col, 1)
    new_momentum = lax.dynamic_update_slice_in_dim(outer_momentum, moment_new, first_col, 1)
    return (new_weights, new_base, new_momentum)


def fused_kernel(
    step_hbm, plan_hbm, weights_hbm, base_hbm, moment_hbm, batch_hbm, cot_hbm,
    weights, base, moment,
    step_ref, plan_ref, normed, turned, full, cot, total, slopes,
    part_out, part_in, part_far, part_own, sum_out, sum_in,
    shares, shares_in, frag_rows,
    load_sem, gather_send, gather_recv, across_send, across_recv, pass_send, pass_recv,
    part_send, part_recv, sum_send, sum_recv,
    share_send, share_recv, frag_send, frag_recv,
):
    inner, shards, tokens, depth = normed.shape
    halves, width = full.shape[2], full.shape[4]
    replicas, share_rows = shares.shape[0], shares.shape[1]
    inv_width = (shards * depth) ** (-0.5)
    rate = inner_rate * inv_width
    me = lax.axis_index("fsdp")
    my_replica = lax.axis_index("replica")
    chip, core = me // 2, me % 2
    partner = chip * 2 + (1 - core)
    across = (1 - chip) * 2 + core
    diagonal = (1 - chip) * 2 + (1 - core)

    def peer(offset):
        return lax.rem(my_replica + offset, replicas)

    def block_cols(half):
        return pl.ds(half * width, width)

    loads = []

    def load(src, dst):
        copy = pltpu.make_async_copy(src, dst, load_sem.at[len(loads)])
        copy.start()
        loads.append(copy)
        return copy

    piece_rows = depth // PIECES
    load_first = [
        load(
            weights_hbm.at[pl.ds(i * piece_rows, piece_rows), block_cols(0)],
            weights.at[pl.ds(i * piece_rows, piece_rows), block_cols(0)],
        )
        for i in range(PIECES)
    ]
    barrier = pltpu.get_barrier_semaphore()
    for other in (partner, across):
        pl.semaphore_signal(barrier, inc=1, device_id={"fsdp": other}, device_id_type=MESH)
    for offset in range(1, replicas):
        pl.semaphore_signal(barrier, inc=1, device_id={"replica": peer(offset)}, device_id_type=MESH)
    load_rest = [
        load(weights_hbm.at[:, block_cols(h)], weights.at[:, block_cols(h)]) for h in range(1, halves)
    ]
    load_x = [
        [load(batch_hbm.at[k, :, pl.ds(o * depth, depth)], normed.at[k, o]) for o in range(shards)]
        for k in range(inner)
    ]
    load_base = load(base_hbm, base)
    load_moment = load(moment_hbm, moment)
    load_cot = load(cot_hbm, cot)
    load_small = [load(step_hbm, step_ref), load(plan_hbm, plan_ref)]

    started = []

    def send(src, dst, send_sem, recv_sem, target):
        copy = pltpu.make_async_remote_copy(
            src_ref=src, dst_ref=dst, send_sem=send_sem, recv_sem=recv_sem,
            device_id=target, device_id_type=MESH,
        )
        copy.start()
        started.append(copy)
        return copy

    def slot(k, h, i):
        return (k * halves + h) * 2 + i

    gathers, partials, sums = {}, {}, {}
    pieces = [slice(i * piece_rows, (i + 1) * piece_rows) for i in range(PIECES)]

    def piece_slot(k, h, i):
        return (k * halves + h) * PIECES + i

    def cast_rows(k, h, rows):
        full[k, me, h, rows, :] = weights[rows, h * width : (h + 1) * width].astype(jnp.bfloat16)

    def gather_across(k, h, i):
        mine = full.at[k, me, h, pl.ds(i * piece_rows, piece_rows), :]
        at = piece_slot(k, h, i)
        gathers[k, h, "across", i] = send(mine, mine, across_send.at[at], across_recv.at[at], {"fsdp": across})

    def gather_beside(k, h):
        mine = full.at[k, me, h]
        at = k * halves + h
        gathers[k, h, "beside"] = send(mine, mine, gather_send.at[at], gather_recv.at[at], {"fsdp": partner})

    def normalize_rows(k):
        rows = 16

        @pl.loop(0, tokens // rows)
        def _(i):
            at = pl.ds(pl.multiple_of(i * rows, rows), rows)
            squares = jnp.zeros((rows, 1), jnp.float32)
            for o in range(shards):
                x = normed[k, o, at, :].astype(jnp.float32)
                squares = squares + jnp.sum(x * x, axis=-1, keepdims=True)
            scale = lax.rsqrt(squares * (1.0 / (shards * depth)) + eps_norm)
            for o in range(shards):
                x = normed[k, o, at, :].astype(jnp.float32)
                normed[k, o, at, :] = (x * scale).astype(jnp.bfloat16)

    tile = 256

    def turn(k):
        for o in range(shards):

            @pl.loop(0, depth // tile)
            def _(b):
                at = pl.ds(pl.multiple_of(b * tile, tile), tile)
                turned[o, at, :] = normed[k, o, :, at].T

    def forward(k, h):
        def term(owner):
            return jnp.dot(normed[k, owner], full[k, owner, h], preferred_element_type=jnp.float32)

        passed = []
        for i in range(PIECES):
            gathers[k, h, "across", i].wait_recv()
            theirs = full.at[k, across, h, pl.ds(i * piece_rows, piece_rows), :]
            at = piece_slot(k, h, i)
            passed.append(send(theirs, theirs, pass_send.at[at], pass_recv.at[at], {"fsdp": partner}))
        total[...] = term(me)
        gathers[k, h, "beside"].wait_recv()
        total[...] += term(partner)
        total[...] += term(across)
        for copy in passed:
            copy.wait_recv()
        values = (total[...] + term(diagonal)) * inv_width
        cot_rows = cot[k, :, h * width : (h + 1) * width].astype(jnp.float32)
        slopes[...] = (cot_rows * silu_slope(values)).astype(jnp.bfloat16)

    def product(owner, dst):
        @pl.loop(0, depth // tile)
        def _(b):
            at = pl.ds(pl.multiple_of(b * tile, tile), tile)
            dst[at, :] = jnp.dot(
                turned[owner, at, :], slopes[...], preferred_element_type=jnp.float32
            ).astype(jnp.bfloat16)

    def gradient_start(k, h):
        def hand_over(i, owner):
            product(owner, part_out.at[k, h, i])
            return send(
                part_out.at[k, h, i], part_in.at[k, h, i],
                part_send.at[slot(k, h, i)], part_recv.at[slot(k, h, i)], {"fsdp": partner},
            )

        sent = [hand_over(0, diagonal)]
        product(across, part_far)
        sent[0].wait_recv()
        for i, rows in enumerate(pieces):
            sum_out[k, h, rows, :] = (
                part_far[rows, :].astype(jnp.float32) + part_in[k, h, 0, rows, :].astype(jnp.float32)
            ).astype(jnp.bfloat16)
            piece = pl.ds(i * piece_rows, piece_rows)
            at = piece_slot(k, h, i)
            sums[k, h, i] = send(
                sum_out.at[k, h, piece, :], sum_in.at[k, h, piece, :],
                sum_send.at[at], sum_recv.at[at], {"fsdp": across},
            )
        sent.append(hand_over(1, partner))
        partials[k, h] = sent
        product(me, part_own.at[h])

    def gradient_finish(k, h):
        partials[k, h][1].wait_recv()
        cols = slice(h * width, (h + 1) * width)
        near = part_own[h].astype(jnp.float32) + part_in[k, h, 1].astype(jnp.float32)
        weights[:, cols] = weights[:, cols] - rate * near
        for i, rows in enumerate(pieces):
            sums[k, h, i].wait_recv()
            if k + 1 < inner:
                weights[rows, cols] = weights[rows, cols] - rate * sum_in[k, h, rows, :].astype(jnp.float32)
                cast_rows(k + 1, h, rows)
                gather_across(k + 1, h, i)
            else:
                blend(h, i)

    fragments = base.shape[1] // HEAD_DIM

    def chosen(rows, index):
        fragment = plan_ref[lax.rem(step_ref[0], SCHED_LEN)]
        return jnp.full((rows, HEAD_DIM), fragment, jnp.int32) == index

    def pick(ref, at, rows):
        found = ref[at, 0:HEAD_DIM]
        for j in range(1, fragments):
            found = jnp.where(chosen(rows, j), ref[at, j * HEAD_DIM : (j + 1) * HEAD_DIM], found)
        return found

    def share_at(r):
        return pl.ds(pl.multiple_of(r * share_rows, share_rows), share_rows)

    def share_start():
        @pl.loop(0, replicas)
        def _(r):
            at = share_at(r)
            pseudo_grad = pick(base, at, share_rows) - pick(weights, at, share_rows)
            top = jnp.max(jnp.abs(pseudo_grad), axis=1, keepdims=True) + eps_scale
            scale = jnp.broadcast_to(top, pseudo_grad.shape).astype(jnp.bfloat16).astype(jnp.float32)
            codes = (pseudo_grad / scale).astype(jnp.bfloat16).astype(jnp.float32)
            shares[r] = codes * scale

        return [
            send(
                shares.at[peer(t)], shares_in.at[t - 1],
                share_send.at[t - 1], share_recv.at[t - 1], {"replica": peer(t)},
            )
            for t in range(1, replicas)
        ]

    def fragment_start(sent):
        running = shares[my_replica]
        for t in range(1, replicas):
            sent[t - 1].wait_recv()
            running = running + shares_in[t - 1]
        average = running / replicas
        outer_lr = (outer_rate * 1024.0) / (
            1024.0 + jnp.full((share_rows, HEAD_DIM), step_ref[0], jnp.int32).astype(jnp.float32)
        )
        everything = slice(0, share_rows)
        moment_new = outer_decay * pick(moment, everything, share_rows) + average
        frag_rows[my_replica] = pick(base, share_at(my_replica), share_rows) - outer_lr * (
            outer_decay * moment_new + average
        )
        for j in range(fragments):
            cols = slice(j * HEAD_DIM, (j + 1) * HEAD_DIM)
            moment[:, cols] = jnp.where(chosen(share_rows, j), moment_new, moment[:, cols])
        return [
            send(
                frag_rows.at[my_replica], frag_rows.at[my_replica],
                frag_send.at[t - 1], frag_recv.at[t - 1], {"replica": peer(t)},
            )
            for t in range(1, replicas)
        ]

    def fragment_finish(sent):
        for copy in sent:
            copy.wait_recv()

        @pl.loop(0, replicas)
        def _(r):
            at = share_at(r)
            for j in range(fragments):
                cols = slice(j * HEAD_DIM, (j + 1) * HEAD_DIM)
                base[at, cols] = jnp.where(chosen(share_rows, j), frag_rows[r], base[at, cols])

    def blend(h, i):
        held = piece_rows // share_rows

        @pl.loop(i * held, (i + 1) * held)
        def _(r):
            at = share_at(r)
            for j in range(h * width // HEAD_DIM, (h + 1) * width // HEAD_DIM):
                cols = slice(j * HEAD_DIM, (j + 1) * HEAD_DIM)
                far = sum_in[inner - 1, h, at, j * HEAD_DIM - h * width : (j + 1) * HEAD_DIM - h * width]
                trained = weights[at, cols] - rate * far.astype(jnp.float32)
                mixed = mix_local * trained + (1.0 - mix_local) * frag_rows[r]
                weights[at, cols] = jnp.where(chosen(share_rows, j), mixed, trained)

    pl.semaphore_wait(barrier, replicas + 1)
    for i, rows in enumerate(pieces):
        load_first[i].wait()
        cast_rows(0, 0, rows)
        gather_across(0, 0, i)
    gather_beside(0, 0)
    for h in range(1, halves):
        load_rest[h - 1].wait()
        cast_rows(0, h, slice(0, depth))
        gather_beside(0, h)
    for copy in load_x[0]:
        copy.wait()
    normalize_rows(0)
    for i in range(PIECES // 2):
        ahead = gathers[0, 0, "across", i]
        ahead.wait_send()
        started.remove(ahead)
    for h in range(1, halves):
        for i in range(PIECES):
            gather_across(0, h, i)
    turn(0)
    load_cot.wait()
    for k in range(inner):
        for h in range(halves):
            forward(k, h)
            gradient_start(k, h)
            if h > 0:
                continue
            if k == 0:
                for copy in load_x[1]:
                    copy.wait()
                normalize_rows(1)
            else:
                fragment_finish(frag_sent)
        if k == 0:
            for copy in load_small:
                copy.wait()
            load_base.wait()
            share_sent = share_start()
        for h in range(halves):
            gradient_finish(k, h)
            if k + 1 < inner:
                gather_beside(k + 1, h)
            if k == 0 and h == 0:
                turn(1)
        if k == 0:
            load_moment.wait()
            frag_sent = fragment_start(share_sent)
    for copy in started:
        copy.wait_send()


def fused(local_weights, outer_base, outer_momentum, batch, cotangent, step, plan):
    rows, columns = outer_base.shape
    inner, tokens, features = batch.shape[1:]
    shards, replicas = features // rows, rows // outer_momentum.shape[0]
    share_rows = outer_momentum.shape[0]
    halves = 2
    width = columns // halves
    f32, bf16 = jnp.float32, jnp.bfloat16
    hbm = pl.BlockSpec(memory_space=pltpu.HBM)
    dma = pltpu.SemaphoreType.DMA
    flops = inner * 4 * tokens * features * columns
    return pl.pallas_call(
        fused_kernel,
        out_shape=(
            pltpu.VMEM((rows, columns), f32),
            pltpu.VMEM((rows, columns), f32),
            pltpu.VMEM((share_rows, columns), f32),
        ),
        in_specs=[hbm] * 7,
        out_specs=(pl.BlockSpec(memory_space=pltpu.VMEM),) * 3,
        scratch_shapes=[
            pltpu.SMEM(step.shape, jnp.int32),
            pltpu.SMEM(plan.shape, jnp.int32),
            pltpu.VMEM((inner, shards, tokens, rows), bf16),
            pltpu.VMEM((shards, rows, tokens), bf16),
            pltpu.VMEM((inner, shards, halves, rows, width), bf16),
            pltpu.VMEM((inner, tokens, columns), bf16),
            pltpu.VMEM((tokens, width), f32),
            pltpu.VMEM((tokens, width), bf16),
            pltpu.VMEM((inner, halves, 2, rows, width), bf16),
            pltpu.VMEM((inner, halves, 2, rows, width), bf16),
            pltpu.VMEM((rows, width), bf16),
            pltpu.VMEM((halves, rows, width), bf16),
            pltpu.VMEM((inner, halves, rows, width), bf16),
            pltpu.VMEM((inner, halves, rows, width), bf16),
            pltpu.VMEM((replicas, share_rows, HEAD_DIM), f32),
            pltpu.VMEM((replicas - 1, share_rows, HEAD_DIM), f32),
            pltpu.VMEM((replicas, share_rows, HEAD_DIM), f32),
            dma((PIECES + halves - 1 + inner * shards + 5,)),
            dma((inner * halves,)),
            dma((inner * halves,)),
            dma((inner * halves * PIECES,)),
            dma((inner * halves * PIECES,)),
            dma((inner * halves * PIECES,)),
            dma((inner * halves * PIECES,)),
            dma((inner * halves * 2,)),
            dma((inner * halves * 2,)),
            dma((inner * halves * PIECES,)),
            dma((inner * halves * PIECES,)),
            dma((replicas - 1,)),
            dma((replicas - 1,)),
            dma((replicas - 1,)),
            dma((replicas - 1,)),
        ],
        compiler_params=pltpu.CompilerParams(
            collective_id=0, has_side_effects=True, vmem_limit_bytes=52 * 2**20
        ),
        cost_estimate=pl.CostEstimate(
            flops=flops, bytes_accessed=20 * 2**20, transcendentals=inner * tokens * columns
        ),
    )(step, plan, local_weights[0], outer_base, outer_momentum, batch[0], cotangent[0])


def on_device_fused(*args):
    new_weights, new_base, new_momentum = fused(*args)
    return (new_weights[None], new_base, new_momentum)


def fits(mesh):
    shards, replicas = mesh.shape["fsdp"], mesh.shape["replica"]
    return shards == 4 and replicas % PIECES == 0 and (D // (shards * replicas)) % 8 == 0


def solution(mesh):
    placed = (
        P("replica", "fsdp", None),
        P("fsdp", None),
        P(("fsdp", "replica"), None),
        P("replica", None, "fsdp", None),
        P("replica", None, "fsdp", None),
        P(),
        P(),
    )
    return jax.shard_map(
        on_device_fused if fits(mesh) else on_device,
        mesh=mesh,
        in_specs=placed,
        out_specs=(P("replica", "fsdp", None), P("fsdp", None), P(("fsdp", "replica"), None)),
        check_vma=False,
    )
```
